128 devices in a mesh: rows: 32 (over z, x_hi, y), inst: 4 (over x_lo, core).
Axes of the slice: x: 4 (x_hi: 2, x_lo: 2; x = x_hi * 2 + x_lo), y: 4, z: 4, core: 2. Of those that a mesh axis runs over, the one named last changes fastest.
Arguments:
- adjoint: float32 [8, 5, 589824], P('inst', None, 'rows'), may hold values from -6 to 6
- jacobian: bfloat16 [8, 5, 5, 589824], P('inst', None, None, 'rows'), may hold values from -3 to 3
- source_term: float32 [8, 5, 589824], P('inst', None, 'rows'), may hold values from -6 to 6
- face_area: float32 [131072], P('rows'), may hold values from 0.5 to 8
- face_band: int32 [131072], P('rows'), may hold values from 0 to 199, as said below
- partition_row: int32 [32], P('rows'), may hold values from 0 to 4, as said below
Outputs:
- updated: float32 [8, 5, 589824], P('inst', None, 'rows')
The draws below stay inside these ranges and needn't reach their ends.
Inputs may be any that keep to these rules, and one draw needn't show every extreme that they name: `face_band`: each half of a partition's face slots names every band of its plane at least once. `partition_row`: every blade row 0 .. 4 owns at least one partition.
All inputs are finite; a program needn't handle non-finite values.
Results may differ from the reference program's by a relative error of at most 0.0003.
Values sent between devices are 32-bit elements; how exact they have to be, the bound alone decides.
A program may use at most 128 MiB of HBM per device.

```python
import math
import jax
import jax.numpy as jnp
from jax import lax

NT = 8
NV = 5
NB = 200
PLANES = 4
CELLS_DEV = 18432
FACE_DEV = 4096
PB = 800
CELLS = 589824
FACES = 131072
N_ROWS = 32


def draw_face_band(key, part):
    key = jax.random.fold_in(key, 11)
    halves = 2 * N_ROWS
    half_len = FACE_DEV // 2
    keys = jax.random.split(key, halves + 2)
    orders = jax.vmap(lambda k: jax.random.permutation(k, NB))(keys[:halves])
    first = jax.random.randint(keys[halves], (halves, half_len), 0, NB)
    second = jax.random.randint(keys[halves + 1], (halves, half_len), 0, NB)
    skewed = jnp.minimum(first, second)
    position = jnp.arange(half_len)
    indices = jnp.broadcast_to(jnp.minimum(position, NB - 1)[None, :], (halves, half_len))
    picked = jnp.take_along_axis(orders, indices, axis=1)
    result = jnp.where(position[None, :] < NB, picked, skewed)
    return result.reshape(FACES).astype(jnp.int32)


def draw_partition_row(key, part):
    key = jax.random.fold_in(key, 23)
    first, second = jax.random.split(key)
    index = jnp.arange(N_ROWS)
    extra = jax.random.randint(first, (N_ROWS,), 0, PLANES + 1)
    base = jnp.where(index < PLANES + 1, index, extra)
    return jax.random.permutation(second, base).astype(jnp.int32)


def shard_levels(key, extent, shards, smallest, largest):
    def one(dim, parts):
        steps = jax.random.uniform(jax.random.fold_in(jax.random.fold_in(key, 6), dim), (parts,), jnp.float32, smallest / len(shards), largest / len(shards))
        return jnp.repeat(jnp.exp(steps), extent[dim] // parts).reshape((-1,) + (1,) * (len(extent) - dim - 1))

    level = one(*shards[0])
    for cut in shards[1:]:
        level = level * one(*cut)
    return level


def normal_values(rng, extent, width, most, shards=(), dtype=jnp.bfloat16):
    level = shard_levels(rng, extent, shards, -0.22, 0.18) if shards else 1.0
    values = jax.random.normal(rng, extent, jnp.float32) * width * level
    return jnp.minimum(jnp.maximum(values, -most), most).astype(dtype)


def setup_inputs(seed: int = 0) -> dict:
    seeds = jax.random.split(jax.random.key(seed), 7)
    return {
        "adjoint": normal_values(seeds[0], (NT, NV, CELLS), 1.0, 6.0, ((0, 4), (2, 32)), jnp.float32),
        "jacobian": normal_values(seeds[1], (NT, NV, NV, CELLS), 0.45, 3.0, ((0, 4), (3, 32))),
        "source_term": normal_values(seeds[2], (NT, NV, CELLS), 1.0, 6.0, ((0, 4), (2, 32)), jnp.float32),
        "face_area": jnp.clip(jnp.exp(math.log(8.0) - 2.7725887 * jax.random.uniform(seeds[3], (FACES,), jnp.float32) ** shard_levels(seeds[3], (FACES,), ((0, 32),), -0.2, 0.2)), 0.5, 8.0),
        "face_band": draw_face_band(jax.random.fold_in(seeds[6], 71), 0),
        "partition_row": draw_partition_row(jax.random.fold_in(seeds[6], 71), 0),
    }


frequency = 1.0
coupling_gain = 2.0
pseudo_step = 0.5


def spectral_matrix():
    index = jnp.arange(NT)
    offset_int = index[:, None] - index[None, :]
    offset = offset_int.astype(jnp.float32)
    safe = jnp.where(offset_int == 0, 1.0, offset)
    parity = jnp.where(jnp.abs(offset_int) % 2 == 0, 1.0, -1.0)
    return jnp.where(offset_int == 0, 0.0, 0.5 * parity / jnp.tan(math.pi * safe / NT)).astype(jnp.float32)


def band_ids(bands_here, owner):
    position = jnp.arange(FACE_DEV)
    plane = jnp.where(position < FACE_DEV // 2, jnp.maximum(owner - 1, 0), jnp.minimum(owner, PLANES - 1))
    return (plane * NB + bands_here).astype(jnp.int32)


def one_hot(identity):
    return (identity[:, None] == jnp.arange(PB)[None, :]).astype(jnp.float32)


def reference(adjoint, jacobian, source_term, face_area, face_band, partition_row):
    flux = jnp.sum(jacobian.astype(jnp.float32) * adjoint[:, :, None, :], axis=1)
    coupled = frequency * jnp.einsum("st,svc->tvc", spectral_matrix(), adjoint, precision=lax.Precision.HIGHEST)
    blocks = adjoint.reshape(NT, NV, N_ROWS, CELLS_DEV)[..., CELLS_DEV - FACE_DEV:]
    face_values = jnp.transpose(blocks, (2, 0, 1, 3)).reshape(N_ROWS, NT * NV, FACE_DEV)
    area_rows = face_area.reshape(N_ROWS, FACE_DEV)
    band_rows = face_band.reshape(N_ROWS, FACE_DEV)

    def accumulate(carry, items):
        values, area, bands_here, owner = items
        table = one_hot(band_ids(bands_here, owner))
        partial_value = carry[0] + jnp.dot(values * area[None, :], table, precision=lax.Precision.HIGHEST)
        weight = carry[1] + jnp.dot(area, table, precision=lax.Precision.HIGHEST)
        return (partial_value, weight), None

    start = (jnp.zeros((NT * NV, PB), jnp.float32), jnp.zeros((PB,), jnp.float32))
    (partial_value, weight), unused = lax.scan(accumulate, start, (face_values, area_rows, band_rows, partition_row))
    means = partial_value / weight[None, :]

    def couple(items):
        values, bands_here, owner = items
        table = one_hot(band_ids(bands_here, owner))
        face_mean = jnp.dot(means, table.T, precision=lax.Precision.HIGHEST)
        return coupling_gain * (face_mean - values)

    mixing = lax.map(couple, (face_values, band_rows, partition_row))
    mixing = jnp.transpose(mixing.reshape(N_ROWS, NT, NV, FACE_DEV), (1, 2, 0, 3))
    residual = (flux + coupled - source_term).reshape(NT, NV, N_ROWS, CELLS_DEV)
    residual = jnp.concatenate([residual[..., :CELLS_DEV - FACE_DEV], residual[..., CELLS_DEV - FACE_DEV:] + mixing], axis=3)
    return adjoint - pseudo_step * residual.reshape(NT, NV, CELLS)
```

```python
import jax
import jax.numpy as jnp
import numpy as np
from jax import lax
from jax.experimental import pallas as pl
from jax.experimental.pallas import tpu as pltpu
from jax.sharding import PartitionSpec as P

MESH = pl.DeviceIdType.MESH
NT = 8
NV = 5
NB = 200
PLANES = 4
BANDS = 256
LANES = 128

frequency = 1.0
coupling_gain = 2.0
pseudo_step = 0.5

GROUP = 4
CHUNKS = 9
RAW = 1
OWNERS = 16


def spectral(offset):
    if offset % NT == 0:
        return 0.0
    angle = np.float32(np.pi * offset / NT)
    return float(np.float32(0.5 * (-1) ** (offset % 2)) / np.tan(angle))


def weight_of(offset):
    return -pseudo_step * frequency * spectral(offset)


def pick(first, up, down):
    return jnp.where(first, jnp.float32(up), jnp.float32(down))


def swap(x):
    even = lax.broadcasted_iota(jnp.int32, x.shape, x.ndim - 2) % 2 == 0
    return jnp.where(even, pltpu.roll(x, 7, x.ndim - 2), pltpu.roll(x, 1, x.ndim - 2))


def split(x):
    high = x.astype(jnp.bfloat16)
    low = (x - high.astype(jnp.float32)).astype(jnp.bfloat16)
    return jnp.concatenate([high, low], axis=0)


def kernel(
    adjoint, jacobian, source, area, band, owner, updated,
    own, jac, src, sibling, result, outbox, inbox, relay, area_v, band_v,
    table, weighted, part, gathered, half_sum, other_sum, totals,
    local_sem, result_sem, sib_send, sib_recv, link_send, link_recv, relay_send, relay_recv,
    rs_send, rs_recv, x_send, x_recv, ag_send, ag_recv,
):
    rows, inst = lax.axis_index("rows"), lax.axis_index("inst")
    z, x_hi, y = rows // 8, (rows // 4) % 2, rows % 4
    first_core = inst % 2 == 0
    sibling_id = (rows, inst + 1 - 2 * (inst % 2))
    link_id = (rows, (inst + 2) % 4)
    across_id = (z * 8 + (1 - x_hi) * 4 + y, inst)
    me = z * 4 + y
    faces = weighted.shape[1]
    half = faces // 2
    face_groups = faces // (4 * LANES)
    face_start = GROUP * CHUNKS - face_groups

    def place(k):
        return (z + k // 4) % 4, (y + k % 4) % 4

    def device(k):
        zd, yd = place(k)
        return (zd * 8 + x_hi * 4 + yd, inst)

    def span(c):
        return pl.ds(c * GROUP, GROUP)

    def each(low, high, act):
        def body(k, carry):
            act(k)
            return carry

        lax.fori_loop(low, high, body, 0)

    def fetch(k, a, b):
        copy = pltpu.make_async_copy(a, b, local_sem.at[k])
        copy.start()
        return copy

    got_area = fetch(0, area, area_v)
    got_band = fetch(1, band, band_v)
    tail, front = pl.ds(face_start, face_groups), pl.ds(0, face_start)
    got_faces = fetch(3, adjoint.at[:, tail], own.at[:, tail])
    got_front = fetch(4, adjoint.at[:, front], own.at[:, front])
    got_jac = fetch(5, jacobian, jac)
    got_src = fetch(6, source, src)

    barrier = pltpu.get_barrier_semaphore()

    def announce(device_id):
        pl.semaphore_signal(barrier, inc=1, device_id=device_id, device_id_type=MESH)

    for partner in (sibling_id, link_id, across_id):
        announce(partner)
    each(1, OWNERS, lambda k: announce(device(k)))

    got_area.wait()
    got_band.wait()
    got_faces.wait()
    band_index = lax.broadcasted_iota(jnp.int32, (BANDS, LANES), 0)
    weighted[...] = jnp.zeros_like(weighted)

    def weigh(g):
        for r in range(4):
            tile = 4 * g + r
            here = pl.ds(pl.multiple_of(tile * LANES, LANES), LANES)
            size = area_v[pl.ds(tile, 1), :]
            for v in range(NV):
                weighted[2 * v : 2 * v + 2, here] = own[v, face_start + g, 2 * r : 2 * r + 2, :] * size
            weighted[2 * NV : 2 * NV + 1, here] = size
            table[:, here] = jnp.where(band_index == band_v[pl.ds(tile, 1), :], 1.0, 0.0).astype(jnp.bfloat16)

    each(0, face_groups, weigh)

    row = owner[0]
    planes = (jnp.maximum(row - 1, 0), jnp.minimum(row, PLANES - 1))
    on_plane = [
        [jnp.where(planes[h] == p, jnp.float32(1), jnp.float32(0)) for p in range(PLANES)]
        for h in range(2)
    ]
    sums = []
    for h in range(2):
        cut = slice(h * half, (h + 1) * half)
        both = lax.dot_general(
            split(weighted[:, cut]), table[:, cut], (((1,), (1,)), ((), ())),
            preferred_element_type=jnp.float32,
        )
        sums.append(both[0:16] + both[16:32])
    for p in range(PLANES):
        here = sums[0] * on_plane[0][p] + sums[1] * on_plane[1][p]
        for q in range(4):
            part[4 * p + q] = here[8 * (q // 2) : 8 * (q // 2) + 8, LANES * (q % 2) : LANES * (q % 2 + 1)]

    pl.semaphore_wait(barrier, OWNERS + 2)

    def remote(a, b, send, recv, device_id):
        return pltpu.make_async_remote_copy(
            a, b, send, recv, device_id=device_id, device_id_type=MESH
        )

    def raw_to_link(c):
        return remote(own.at[:, span(c)], inbox.at[:, span(c)], link_send.at[c], link_recv.at[c], link_id)

    def to_link(c):
        return remote(outbox.at[:, span(c)], inbox.at[:, span(c)], link_send.at[c], link_recv.at[c], link_id)

    def to_sibling(c):
        return remote(own.at[:, span(c)], sibling.at[:, span(c)], sib_send.at[c], sib_recv.at[c], sibling_id)

    def to_relay(c):
        return remote(inbox.at[:, span(c)], relay.at[:, span(c)], relay_send.at[c], relay_recv.at[c], sibling_id)

    def scatter(k):
        zd, yd = place(k)
        return remote(part.at[zd * 4 + yd], gathered.at[k], rs_send.at[k], rs_recv.at[k], device(k))

    def gather(k):
        return remote(totals.at[me], totals.at[me], ag_send.at[k], ag_recv.at[k], device(k))

    across = remote(half_sum, other_sum, x_send, x_recv, across_id)

    got_front.wait()
    each(0, RAW, lambda c: raw_to_link(c).start())
    each(1, OWNERS, lambda k: scatter(k).start())
    each(0, CHUNKS, lambda c: to_sibling(c).start())

    odd = lax.broadcasted_iota(jnp.int32, (8, LANES), 0) % 2 == 1

    def weights(by_offset):
        return by_offset[0], jnp.where(odd, by_offset[1], by_offset[-1])

    shifts = (-1, 0, 1)
    inner = weights({d: weight_of(d) for d in shifts})
    facing = weights({d: weight_of(4 + d) for d in shifts})
    near = weights({d: pick(first_core, weight_of(2 + d), weight_of(-2 + d)) for d in shifts})
    away = weights({d: pick(first_core, weight_of(-2 + d), weight_of(2 + d)) for d in shifts})

    def combine(a, b, wa, wb):
        return wa[0] * a + wb[0] * b + swap(wa[1] * a + wb[1] * b)

    def send_partial(c):
        to_sibling(c).wait_recv()
        for v in range(NV):
            outbox[v, span(c)] = combine(own[v, span(c)], sibling[v, span(c)], facing, away)
        to_link(c).start()

    each(0, RAW, lambda c: to_sibling(c).wait_recv())
    each(RAW, CHUNKS, send_partial)

    got_jac.wait()
    got_src.wait()

    def base(c):
        here = span(c)
        half_groups = pl.ds(c * (GROUP // 2), GROUP // 2)
        state = [own[w, here] for w in range(NV)]
        for v in range(NV):
            flux = 0.0
            for w in range(NV):
                block = jac[w, v, half_groups].astype(jnp.float32).reshape(GROUP, 8, LANES)
                flux = flux + block * state[w]
            coupled = combine(state[v], sibling[v, here], inner, near)
            result[v, here] = state[v] + coupled - pseudo_step * (flux - src[v, here])

    each(0, CHUNKS, base)

    each(1, OWNERS, lambda k: scatter(k).wait())
    total = part[me]
    for k in range(1, OWNERS):
        total = total + gathered[k]
    half_sum[...] = total
    across.start()

    def pass_on(c):
        raw_to_link(c).wait_recv()
        to_relay(c).start()

    each(0, RAW, pass_on)

    across.wait()
    totals[me] = half_sum[...] + other_sum[...]
    each(1, OWNERS, lambda k: gather(k).start())

    def to_result(c):
        return pltpu.make_async_copy(result.at[:, span(c)], updated.at[:, span(c)], result_sem.at[c])

    def finish_raw(c):
        to_relay(c).wait()
        for v in range(NV):
            result[v, span(c)] += combine(inbox[v, span(c)], relay[v, span(c)], facing, away)
        to_result(c).start()

    each(0, RAW, finish_raw)

    def finish(c):
        to_link(c).wait_recv()
        result[:, span(c)] += inbox[:, span(c)]
        to_result(c).start()

    each(RAW, face_start // GROUP, finish)

    each(1, OWNERS, lambda k: gather(k).wait())
    for h in range(2):
        top, bottom = 0.0, 0.0
        for p in range(PLANES):
            tile = [totals[4 * p + q] for q in range(4)]
            top = top + jnp.concatenate(tile[0:2], axis=1) * on_plane[h][p]
            bottom = bottom + jnp.concatenate(tile[2:4], axis=1) * on_plane[h][p]
        total_area = bottom[2:3]
        total_area = jnp.where(total_area > 0, total_area, 1.0)
        means = split(jnp.concatenate([top / total_area, bottom / total_area], axis=0))
        cut = slice(h * half, (h + 1) * half)
        both = jnp.dot(means, table[:, cut], preferred_element_type=jnp.float32)
        weighted[:, cut] = (both[0:16] + both[16:32]) * (pseudo_step * coupling_gain)

    def mix(g):
        here = face_start + g
        for v in range(NV):
            result[v, here] += own[v, here] * (pseudo_step * coupling_gain)
            for r in range(4):
                lanes = pl.ds(pl.multiple_of((4 * g + r) * LANES, LANES), LANES)
                result[v, here, 2 * r : 2 * r + 2, :] -= weighted[2 * v : 2 * v + 2, lanes]

    each(0, face_groups, mix)
    each(face_start // GROUP, CHUNKS, finish)

    each(0, CHUNKS, lambda c: to_result(c).wait())
    each(0, CHUNKS, lambda c: to_sibling(c).wait_send())
    each(0, RAW, lambda c: raw_to_link(c).wait_send())
    each(RAW, CHUNKS, lambda c: to_link(c).wait_send())


def fold(x):
    cells = x.shape[2]
    x = x.reshape(2, NV, cells // (4 * LANES), 4, LANES).transpose(1, 2, 3, 0, 4)
    return x.reshape(NV, cells // (4 * LANES), 8, LANES)


def unfold(x):
    x = x.reshape(NV, x.shape[1], 4, 2, LANES).transpose(3, 0, 1, 2, 4)
    return x.reshape(2, NV, -1)


def fold_jacobian(x):
    cells = x.shape[3]
    x = x.reshape(2, NV, NV, cells // (8 * LANES), 8, LANES).transpose(1, 2, 3, 4, 0, 5)
    return x.reshape(NV, NV, cells // (8 * LANES), 16, LANES)


def shards(adjoint, jacobian, source_term, face_area, face_band, partition_row):
    cells, faces = adjoint.shape[2], face_area.shape[0]
    groups = cells // (4 * LANES)
    assert groups == GROUP * CHUNKS
    f32, bf16, i32 = jnp.float32, jnp.bfloat16, jnp.int32
    dma = pltpu.SemaphoreType.DMA
    state = pltpu.VMEM((NV, groups, 8, LANES), f32)
    tile = pltpu.VMEM((8, LANES), f32)
    tiles = pltpu.VMEM((OWNERS, 8, LANES), f32)
    updated = pl.pallas_call(
        kernel,
        out_shape=jax.ShapeDtypeStruct((NV, groups, 8, LANES), f32),
        in_specs=[pl.BlockSpec(memory_space=pl.ANY)] * 5 + [pl.BlockSpec(memory_space=pltpu.SMEM)],
        out_specs=pl.BlockSpec(memory_space=pl.ANY),
        scratch_shapes=[
            state,
            pltpu.VMEM((NV, NV, groups // 2, 16, LANES), bf16),
            state,
            state,
            state,
            state,
            state,
            pltpu.VMEM((NV, RAW * GROUP, 8, LANES), f32),
            pltpu.VMEM((faces // LANES, LANES), f32),
            pltpu.VMEM((faces // LANES, LANES), i32),
            pltpu.VMEM((BANDS, faces), bf16),
            pltpu.VMEM((16, faces), f32),
            tiles,
            tiles,
            tile,
            tile,
            tiles,
            dma((7,)),
            dma((CHUNKS,)),
            dma((CHUNKS,)),
            dma((CHUNKS,)),
            dma((CHUNKS,)),
            dma((CHUNKS,)),
            dma((RAW,)),
            dma((RAW,)),
            dma((OWNERS,)),
            dma((OWNERS,)),
            dma,
            dma,
            dma((OWNERS,)),
            dma((OWNERS,)),
        ],
        compiler_params=pltpu.CompilerParams(
            collective_id=0, has_side_effects=True, vmem_limit_bytes=60 << 20
        ),
    )(
        fold(adjoint),
        fold_jacobian(jacobian),
        fold(source_term),
        face_area.reshape(faces // LANES, LANES),
        face_band.reshape(faces // LANES, LANES),
        partition_row,
    )
    return unfold(updated)


def solution(mesh):
    placed = (
        P("inst", None, "rows"),
        P("inst", None, None, "rows"),
        P("inst", None, "rows"),
        P("rows"),
        P("rows"),
        P("rows"),
    )
    return jax.shard_map(
        shards, mesh=mesh, in_specs=placed, out_specs=P("inst", None, "rows"), check_vma=False
    )
```

```python
import jax
import jax.numpy as jnp
import numpy as np
from jax import lax
from jax.experimental import pallas as pl
from jax.experimental.pallas import tpu as pltpu
from jax.sharding import PartitionSpec as P

MESH = pl.DeviceIdType.MESH
NT = 8
NV = 5
NB = 200
PLANES = 4
BANDS = 256
LANES = 128

frequency = 1.0
coupling_gain = 2.0
pseudo_step = 0.5

GROUP = 4
CHUNKS = 9
RAW = 2
OWNERS = 16


def spectral(offset):
    if offset % NT == 0:
        return 0.0
    angle = np.float32(np.pi * offset / NT)
    return float(np.float32(0.5 * (-1) ** (offset % 2)) / np.tan(angle))


def weight_of(offset):
    return -pseudo_step * frequency * spectral(offset)


def pick(first, up, down):
    return jnp.where(first, jnp.float32(up), jnp.float32(down))


def swap(x):
    even = lax.broadcasted_iota(jnp.int32, x.shape, x.ndim - 2) % 2 == 0
    return jnp.where(even, pltpu.roll(x, 7, x.ndim - 2), pltpu.roll(x, 1, x.ndim - 2))


def split(x):
    high = x.astype(jnp.bfloat16)
    low = (x - high.astype(jnp.float32)).astype(jnp.bfloat16)
    return jnp.concatenate([high, low], axis=0)


def kernel(
    adjoint, jacobian, source, area, band, owner, result,
    own, jac, src, sibling, outbox, inbox, relay, area_v, band_v,
    table, weighted, part, gathered, half_sum, other_sum, total, means,
    near_sem, local_sem, sib_send, sib_recv, link_send, link_recv, relay_send, relay_recv,
    rs_send, rs_recv, x_send, x_recv, ag_send, ag_recv,
):
    rows, inst = lax.axis_index("rows"), lax.axis_index("inst")
    z, x_hi, y = rows // 8, (rows // 4) % 2, rows % 4
    core = inst % 2
    first, second = core == 0, core == 1
    sibling_id = (rows, inst + 1 - 2 * core)
    link_id = (rows, (inst + 2) % 4)
    diagonal_id = (rows, (inst + 2) % 4 + 1 - 2 * core)
    across_id = (z * 8 + (1 - x_hi) * 4 + y, inst)
    me = z * 4 + y
    faces = weighted.shape[1]
    half = faces // 2
    face_groups = faces // (4 * LANES)
    face_start = GROUP * CHUNKS - face_groups
    face_chunk = face_start // GROUP

    def place(k):
        return (z + k // 4) % 4, (y + k % 4) % 4

    def device(k, inst):
        zd, yd = place(k)
        return (zd * 8 + x_hi * 4 + yd, inst)

    def span(c):
        return pl.ds(c * GROUP, GROUP)

    def each(low, high, act):
        def body(k, carry):
            act(k)
            return carry

        lax.fori_loop(low, high, body, 0)

    def fetch(k, a, b):
        copy = pltpu.make_async_copy(a, b, local_sem.at[k])
        copy.start()
        return copy

    def signal(sem, device_id):
        pl.semaphore_signal(sem, inc=1, device_id=device_id, device_id_type=MESH)

    def remote(a, b, send, recv, device_id):
        return pltpu.make_async_remote_copy(
            a, b, send, recv, device_id=device_id, device_id_type=MESH
        )

    def to_sibling(c):
        return remote(
            adjoint.at[:, span(c)], sibling.at[:, span(c)], sib_send.at[c], sib_recv.at[c], sibling_id
        )

    def to_link(source_ref, c, core_there):
        target = (rows, (inst + 2) % 4 + core_there)
        return remote(
            source_ref.at[:, span(c)], inbox.at[:, span(c)], link_send.at[core_there, c], link_recv.at[c], target
        )

    def to_relay(c):
        return remote(inbox.at[:, span(c)], relay.at[:, span(c)], relay_send.at[c], relay_recv.at[c], sibling_id)

    def scatter(k):
        zd, yd = place(k)
        return remote(part.at[zd * 4 + yd], gathered.at[k], rs_send.at[k], rs_recv.at[k], device(k, inst))

    slot = 2 * z + y % 2
    served = inst - y // 2

    def gather(k):
        return remote(total, means.at[slot], ag_send.at[k], ag_recv.at[slot], device(k, served))

    def keep():
        return pltpu.make_async_copy(total, means.at[slot], ag_recv.at[slot])

    def arrived(n):
        return remote(total, means.at[n], ag_send.at[0], ag_recv.at[n], sibling_id)

    across = remote(half_sum, other_sum, x_send, x_recv, across_id)

    barrier = pltpu.get_barrier_semaphore()

    @pl.when(first)
    def _():
        signal(barrier, link_id)

    @pl.when(second)
    def _():
        signal(barrier, sibling_id)
        signal(barrier, diagonal_id)

    tail, front = pl.ds(face_start, face_groups), pl.ds(0, face_start)
    got_faces = fetch(0, adjoint.at[:, tail], own.at[:, tail])
    got_area = fetch(1, area, area_v)
    got_band = fetch(2, band, band_v)
    got_front = fetch(3, adjoint.at[:, front], own.at[:, front])
    got_jac = fetch(4, jacobian, jac)
    got_src = fetch(5, source, src)

    @pl.when(first)
    def _():
        pl.semaphore_wait(barrier, 3)
        signal(near_sem, sibling_id)
        each(0, RAW, lambda c: to_link(adjoint, c, 0).start())
        each(face_chunk, CHUNKS, lambda c: to_sibling(c).start())
        each(0, face_chunk, lambda c: to_sibling(c).start())

    @pl.when(second)
    def _():
        pl.semaphore_wait(near_sem, 1)
        each(1, OWNERS, lambda k: signal(barrier, device(k, inst)))
        signal(barrier, across_id)
        each(0, CHUNKS, lambda c: to_sibling(c).start())

    got_area.wait()
    got_band.wait()
    band_index = lax.broadcasted_iota(jnp.int32, (BANDS, LANES), 0)

    def mark(n):
        here = pl.ds(pl.multiple_of(n * LANES, LANES), LANES)
        table[:, here] = jnp.where(band_index == band_v[pl.ds(n, 1), :], 1.0, 0.0).astype(jnp.bfloat16)

    row = owner[0]
    planes = (jnp.maximum(row - 1, 0), jnp.minimum(row, PLANES - 1))
    on_plane = [
        [jnp.where(planes[h] == p, jnp.float32(1), jnp.float32(0)) for p in range(PLANES)]
        for h in range(2)
    ]

    def weigh(values, top):
        def group(g):
            for r in range(4):
                tile = 4 * g + r
                here = pl.ds(pl.multiple_of(tile * LANES, LANES), LANES)
                size = area_v[pl.ds(tile, 1), :]
                for v in range(NV):
                    weighted[top + 2 * v : top + 2 * v + 2, here] = (
                        values[v, face_start + g, 2 * r : 2 * r + 2, :] * size
                    )
                weighted[top + 2 * NV : top + 2 * NV + 1, here] = size

        each(0, face_groups, group)

    @pl.when(second)
    def _():
        each(0, faces // LANES, mark)
        weighted[...] = jnp.zeros_like(weighted)
        got_faces.wait()
        weigh(own, 0)
        each(face_chunk, CHUNKS, lambda c: to_sibling(c).wait_recv())
        weigh(sibling, 16)
        sums = []
        for h in range(2):
            cut = slice(h * half, (h + 1) * half)
            both = lax.dot_general(
                split(weighted[:, cut]), table[:, cut], (((1,), (1,)), ((), ())),
                preferred_element_type=jnp.float32,
            )
            sums.append(both[0:32] + both[32:64])
        for p in range(PLANES):
            here = sums[0] * on_plane[0][p] + sums[1] * on_plane[1][p]
            for q in range(4):
                part[4 * p + q] = here[
                    16 * (q // 2) : 16 * (q // 2) + 16, LANES * (q % 2) : LANES * (q % 2 + 1)
                ]
        pl.semaphore_wait(barrier, OWNERS)
        each(1, OWNERS, lambda k: scatter(k).start())

    odd = lax.broadcasted_iota(jnp.int32, (8, LANES), 0) % 2 == 1

    def weights(by_offset):
        return by_offset[0], jnp.where(odd, by_offset[1], by_offset[-1])

    shifts = (-1, 0, 1)
    inner = weights({d: weight_of(d) for d in shifts})
    facing = weights({d: weight_of(4 + d) for d in shifts})
    up = weights({d: weight_of(2 + d) for d in shifts})
    down = weights({d: weight_of(-2 + d) for d in shifts})
    near = weights({d: pick(first, weight_of(2 + d), weight_of(-2 + d)) for d in shifts})
    away = weights({d: pick(first, weight_of(-2 + d), weight_of(2 + d)) for d in shifts})

    def combine(a, b, wa, wb):
        return wa[0] * a + wb[0] * b + swap(wa[1] * a + wb[1] * b)

    @pl.when(first)
    def _():
        got_front.wait()
        got_faces.wait()

        def send_raw(c):
            to_sibling(c).wait_recv()
            to_link(sibling, c, 1).start()

        def send_partial(c):
            to_sibling(c).wait_recv()
            for v in range(NV):
                a, b = own[v, span(c)], sibling[v, span(c)]
                outbox[0, v, span(c)] = combine(a, b, facing, down)
                outbox[1, v, span(c)] = combine(b, a, facing, up)
            to_link(outbox.at[0], c, 0).start()
            to_link(outbox.at[1], c, 1).start()

        each(0, RAW, send_raw)
        each(RAW, CHUNKS, send_partial)
        each(0, faces // LANES, mark)

    @pl.when(second)
    def _():
        each(0, face_chunk, lambda c: to_sibling(c).wait_recv())
        got_front.wait()

    got_jac.wait()
    got_src.wait()

    def base(c):
        here = span(c)
        half_groups = pl.ds(c * (GROUP // 2), GROUP // 2)
        state = [own[w, here] for w in range(NV)]
        for v in range(NV):
            flux = 0.0
            for w in range(NV):
                block = jac[w, v, half_groups].astype(jnp.float32).reshape(GROUP, 8, LANES)
                flux = flux + block * state[w]
            coupled = combine(state[v], sibling[v, here], inner, near)
            result[v, here] = state[v] + coupled - pseudo_step * (flux - src[v, here])

    each(0, CHUNKS, base)

    @pl.when(second)
    def _():
        each(1, OWNERS, lambda k: scatter(k).wait())
        sum_here = part[me]
        for k in range(1, OWNERS):
            sum_here = sum_here + gathered[k]
        half_sum[...] = sum_here
        across.start()
        across.wait()
        total[...] = half_sum[...] + other_sum[...]
        each(1, OWNERS, lambda k: gather(k).start())

        @pl.when(y >= 2)
        def _():
            gather(0).start()

        @pl.when(y < 2)
        def _():
            keep().start()

    def pass_on(c):
        to_link(inbox, c, 0).wait_recv()
        to_relay(c).start()

    each(0, RAW, pass_on)

    def finish_raw(c):
        to_relay(c).wait()
        for v in range(NV):
            result[v, span(c)] += combine(inbox[v, span(c)], relay[v, span(c)], facing, away)

    each(0, RAW, finish_raw)

    def finish(c):
        to_link(inbox, c, 0).wait_recv()
        result[:, span(c)] += inbox[:, span(c)]

    each(RAW, face_chunk, finish)

    each(0, OWNERS // 2, lambda n: arrived(n).wait_recv())
    for h in range(2):
        table_sum = 0.0
        for p in range(PLANES):
            table_sum += jnp.concatenate([means[2 * p], means[2 * p + 1]], axis=1) * on_plane[h][p]
        total_area = table_sum[2 * NV : 2 * NV + 1]
        total_area = jnp.where(total_area > 0, total_area, 1.0)
        cut = slice(h * half, (h + 1) * half)
        both = jnp.dot(split(table_sum / total_area), table[:, cut], preferred_element_type=jnp.float32)
        weighted[0:16, cut] = (both[0:16] + both[16:32]) * (pseudo_step * coupling_gain)

    def mix(g):
        here = face_start + g
        for v in range(NV):
            result[v, here] += own[v, here] * (pseudo_step * coupling_gain)
            for r in range(4):
                lanes = pl.ds(pl.multiple_of((4 * g + r) * LANES, LANES), LANES)
                result[v, here, 2 * r : 2 * r + 2, :] -= weighted[2 * v : 2 * v + 2, lanes]

    each(0, face_groups, mix)
    each(face_chunk, CHUNKS, finish)

    each(0, CHUNKS, lambda c: to_sibling(c).wait_send())

    @pl.when(first)
    def _():
        each(0, CHUNKS, lambda c: to_link(inbox, c, 0).wait_send())
        each(0, CHUNKS, lambda c: to_link(inbox, c, 1).wait_send())

    @pl.when(second)
    def _():
        each(1, OWNERS, lambda k: gather(k).wait_send())

        @pl.when(y >= 2)
        def _():
            gather(0).wait_send()


def hbm(x):
    return pltpu.with_memory_space_constraint(x, pltpu.HBM)


def fold(x):
    cells = x.shape[2]
    x = x.reshape(2, NV, cells // (4 * LANES), 4, LANES).transpose(1, 2, 3, 0, 4)
    return x.reshape(NV, cells // (4 * LANES), 8, LANES)


def unfold(x):
    x = x.reshape(NV, x.shape[1], 4, 2, LANES).transpose(3, 0, 1, 2, 4)
    return x.reshape(2, NV, -1)


def fold_jacobian(x):
    cells = x.shape[3]
    x = x.reshape(2, NV, NV, cells // (8 * LANES), 8, LANES).transpose(1, 2, 3, 4, 0, 5)
    return x.reshape(NV, NV, cells // (8 * LANES), 16, LANES)


def shards(adjoint, jacobian, source_term, face_area, face_band, partition_row):
    cells, faces = adjoint.shape[2], face_area.shape[0]
    groups = cells // (4 * LANES)
    assert groups == GROUP * CHUNKS
    f32, bf16, i32 = jnp.float32, jnp.bfloat16, jnp.int32
    dma = pltpu.SemaphoreType.DMA
    state = pltpu.VMEM((NV, groups, 8, LANES), f32)
    box = pltpu.VMEM((16, LANES), f32)
    boxes = pltpu.VMEM((OWNERS, 16, LANES), f32)
    updated = pl.pallas_call(
        kernel,
        out_shape=pltpu.VMEM((NV, groups, 8, LANES), f32),
        in_specs=[pl.BlockSpec(memory_space=pl.ANY)] * 5 + [pl.BlockSpec(memory_space=pltpu.SMEM)],
        out_specs=pl.BlockSpec(memory_space=pltpu.VMEM),
        scratch_shapes=[
            state,
            pltpu.VMEM((NV, NV, groups // 2, 16, LANES), bf16),
            state,
            state,
            pltpu.VMEM((2, NV, groups, 8, LANES), f32),
            state,
            pltpu.VMEM((NV, RAW * GROUP, 8, LANES), f32),
            pltpu.VMEM((faces // LANES, LANES), f32),
            pltpu.VMEM((faces // LANES, LANES), i32),
            pltpu.VMEM((BANDS, faces), bf16),
            pltpu.VMEM((32, faces), f32),
            boxes,
            boxes,
            box,
            box,
            box,
            pltpu.VMEM((OWNERS // 2, 16, LANES), f32),
            pltpu.SemaphoreType.REGULAR,
            dma((6,)),
            dma((CHUNKS,)),
            dma((CHUNKS,)),
            dma((2, CHUNKS)),
            dma((CHUNKS,)),
            dma((RAW,)),
            dma((RAW,)),
            dma((OWNERS,)),
            dma((OWNERS,)),
            dma,
            dma,
            dma((OWNERS,)),
            dma((OWNERS // 2,)),
        ],
        compiler_params=pltpu.CompilerParams(
            collective_id=0, has_side_effects=True, vmem_limit_bytes=40 << 20
        ),
    )(
        hbm(fold(adjoint)),
        hbm(fold_jacobian(jacobian)),
        hbm(fold(source_term)),
        hbm(face_area.reshape(faces // LANES, LANES)),
        hbm(face_band.reshape(faces // LANES, LANES)),
        partition_row,
    )
    return unfold(updated)


def solution(mesh):
    placed = (
        P("inst", None, "rows"),
        P("inst", None, None, "rows"),
        P("inst", None, "rows"),
        P("rows"),
        P("rows"),
        P("rows"),
    )
    return jax.shard_map(
        shards, mesh=mesh, in_specs=placed, out_specs=P("inst", None, "rows"), check_vma=False
    )
```

```python
import jax
import jax.numpy as jnp
import numpy as np
from jax import lax
from jax.experimental import pallas as pl
from jax.experimental.pallas import tpu as pltpu
from jax.sharding import PartitionSpec as P

MESH = pl.DeviceIdType.MESH
NT = 8
NV = 5
NB = 200
PLANES = 4
BANDS = 256
LANES = 128

frequency = 1.0
coupling_gain = 2.0
pseudo_step = 0.5

GROUP = 4
CHUNKS = 9
RAW = 2
OWNERS = 16


def ring(k):
    return min(k, 4 - k)


FAR_FIRST = sorted(range(1, OWNERS), key=lambda k: -ring(k // 4) - ring(k % 4))


def spectral(offset):
    if offset % NT == 0:
        return 0.0
    angle = np.float32(np.pi * offset / NT)
    return float(np.float32(0.5 * (-1) ** (offset % 2)) / np.tan(angle))


def weight_of(offset):
    return -pseudo_step * frequency * spectral(offset)


def pick(first, up, down):
    return jnp.where(first, jnp.float32(up), jnp.float32(down))


def swap(x):
    even = lax.broadcasted_iota(jnp.int32, x.shape, x.ndim - 2) % 2 == 0
    return jnp.where(even, pltpu.roll(x, 7, x.ndim - 2), pltpu.roll(x, 1, x.ndim - 2))


def split(x):
    high = x.astype(jnp.bfloat16)
    low = (x - high.astype(jnp.float32)).astype(jnp.bfloat16)
    return jnp.concatenate([high, low], axis=0)


def kernel(
    adjoint, jacobian, source, area, band, owner, result,
    own, jac, src, sibling, outbox, inbox, relay, area_v, band_v,
    table, index, weighted, part, gathered, half_sum, other_sum, total, means,
    near_sem, local_sem, sib_send, sib_recv, link_send, link_recv, relay_send, relay_recv,
    rs_send, rs_recv, x_send, x_recv, ag_send, ag_recv,
):
    rows, inst = lax.axis_index("rows"), lax.axis_index("inst")
    z, x_hi, y = rows // 8, (rows // 4) % 2, rows % 4
    core = inst % 2
    first, second = core == 0, core == 1
    sibling_id = (rows, inst + 1 - 2 * core)
    link_id = (rows, (inst + 2) % 4)
    across_id = (z * 8 + (1 - x_hi) * 4 + y, inst)
    me = z * 4 + y
    faces = weighted.shape[1]
    half = faces // 2
    face_groups = faces // (4 * LANES)
    face_start = GROUP * CHUNKS - face_groups
    face_chunk = face_start // GROUP

    def place(k):
        return (z + k // 4) % 4, (y + k % 4) % 4

    def device(k, inst):
        zd, yd = place(k)
        return (zd * 8 + x_hi * 4 + yd, inst)

    def span(c):
        return pl.ds(c * GROUP, GROUP)

    def each(low, high, act):
        def body(k, carry):
            act(k)
            return carry

        lax.fori_loop(low, high, body, 0)

    def fetch(k, a, b):
        copy = pltpu.make_async_copy(a, b, local_sem.at[k])
        copy.start()
        return copy

    def signal(sem, device_id):
        pl.semaphore_signal(sem, inc=1, device_id=device_id, device_id_type=MESH)

    def remote(a, b, send, recv, device_id):
        return pltpu.make_async_remote_copy(
            a, b, send, recv, device_id=device_id, device_id_type=MESH
        )

    def to_sibling(c):
        return remote(
            adjoint.at[:, span(c)], sibling.at[:, span(c)], sib_send.at[c], sib_recv.at[c], sibling_id
        )

    def to_link(source_ref, c, core_there):
        target = (rows, (inst + 2) % 4 + core_there)
        return remote(
            source_ref.at[:, span(c)], inbox.at[:, span(c)], link_send.at[core_there, c], link_recv.at[c], target
        )

    def to_relay(c):
        return remote(inbox.at[:, span(c)], relay.at[:, span(c)], relay_send.at[c], relay_recv.at[c], sibling_id)

    def scatter(k):
        zd, yd = place(k)
        return remote(part.at[zd * 4 + yd], gathered.at[k], rs_send.at[k], rs_recv.at[k], device(k, inst))

    slot = 2 * z + y % 2
    served = inst - y // 2

    def gather(k):
        return remote(total, means.at[slot], ag_send.at[k], ag_recv.at[slot], device(k, served))

    def keep():
        return pltpu.make_async_copy(total, means.at[slot], ag_recv.at[slot])

    def arrived(n):
        return remote(total, means.at[n], ag_send.at[0], ag_recv.at[n], sibling_id)

    across = remote(half_sum, other_sum, x_send, x_recv, across_id)

    barrier = pltpu.get_barrier_semaphore()

    @pl.when(first)
    def _():
        signal(barrier, link_id)

    @pl.when(second)
    def _():
        signal(barrier, sibling_id)
        for k in FAR_FIRST:
            signal(barrier, device(k, inst))
        signal(barrier, across_id)

    tail, front = pl.ds(face_start, face_groups), pl.ds(0, face_start)
    got_faces = fetch(0, adjoint.at[:, tail], own.at[:, tail])
    got_area = fetch(1, area, area_v)
    got_band = fetch(2, band, band_v)
    got_front = fetch(3, adjoint.at[:, front], own.at[:, front])
    got_jac = fetch(4, jacobian, jac)
    got_src = fetch(5, source, src)

    @pl.when(first)
    def _():
        pl.semaphore_wait(barrier, 2)
        signal(near_sem, sibling_id)
        signal(near_sem, link_id)
        each(0, RAW, lambda c: to_link(adjoint, c, 0).start())
        each(face_chunk, CHUNKS, lambda c: to_sibling(c).start())
        each(0, face_chunk, lambda c: to_sibling(c).start())

    @pl.when(second)
    def _():
        pl.semaphore_wait(near_sem, 1)
        each(0, CHUNKS, lambda c: to_sibling(c).start())

    got_area.wait()
    got_band.wait()
    band_index = lax.broadcasted_iota(jnp.int32, (BANDS, LANES), 0)
    block_row = lax.broadcasted_iota(jnp.int32, (8, LANES), 0)

    def locate(g):
        bands = band_v[pl.ds(4 * g, 1), :]
        for r in range(1, 4):
            bands = jnp.where(block_row < 2 * r, bands, band_v[pl.ds(4 * g + r, 1), :])
        index[g] = bands

    def mark(n):
        here = pl.ds(pl.multiple_of(n * LANES, LANES), LANES)
        table[:, here] = jnp.where(band_index == band_v[pl.ds(n, 1), :], 1.0, 0.0).astype(jnp.bfloat16)

    row = owner[0]
    planes = (jnp.maximum(row - 1, 0), jnp.minimum(row, PLANES - 1))
    on_plane = [
        [jnp.where(planes[h] == p, jnp.float32(1), jnp.float32(0)) for p in range(PLANES)]
        for h in range(2)
    ]

    def weigh(values, top):
        def group(g):
            for r in range(4):
                tile = 4 * g + r
                here = pl.ds(pl.multiple_of(tile * LANES, LANES), LANES)
                size = area_v[pl.ds(tile, 1), :]
                for v in range(NV):
                    weighted[top + 2 * v : top + 2 * v + 2, here] = (
                        values[v, face_start + g, 2 * r : 2 * r + 2, :] * size
                    )
                weighted[top + 2 * NV : top + 2 * NV + 1, here] = size

        each(0, face_groups, group)

    @pl.when(second)
    def _():
        each(0, faces // LANES, mark)
        weighted[...] = jnp.zeros_like(weighted)
        got_faces.wait()
        weigh(own, 0)
        each(face_chunk, CHUNKS, lambda c: to_sibling(c).wait_recv())
        weigh(sibling, 16)
        sums = []
        for h in range(2):
            cut = slice(h * half, (h + 1) * half)
            both = lax.dot_general(
                split(weighted[:, cut]), table[:, cut], (((1,), (1,)), ((), ())),
                preferred_element_type=jnp.float32,
            )
            sums.append(both[0:32] + both[32:64])
        for p in range(PLANES):
            here = sums[0] * on_plane[0][p] + sums[1] * on_plane[1][p]
            for q in range(4):
                part[4 * p + q] = here[
                    16 * (q // 2) : 16 * (q // 2) + 16, LANES * (q % 2) : LANES * (q % 2 + 1)
                ]
        pl.semaphore_wait(barrier, OWNERS)
        for k in FAR_FIRST:
            scatter(k).start()

    odd = block_row % 2 == 1

    def weights(by_offset):
        return by_offset[0], jnp.where(odd, by_offset[1], by_offset[-1])

    shifts = (-1, 0, 1)
    inner = weights({d: weight_of(d) for d in shifts})
    facing = weights({d: weight_of(4 + d) for d in shifts})
    up = weights({d: weight_of(2 + d) for d in shifts})
    down = weights({d: weight_of(-2 + d) for d in shifts})
    near = weights({d: pick(first, weight_of(2 + d), weight_of(-2 + d)) for d in shifts})
    away = weights({d: pick(first, weight_of(-2 + d), weight_of(2 + d)) for d in shifts})

    def combine(a, b, wa, wb):
        return wa[0] * a + wb[0] * b + swap(wa[1] * a + wb[1] * b)

    @pl.when(first)
    def _():
        got_front.wait()
        got_faces.wait()

        def send_raw(c):
            to_sibling(c).wait_recv()
            to_link(sibling, c, 1).start()

        def send_partial(c):
            to_sibling(c).wait_recv()
            for v in range(NV):
                a, b = own[v, span(c)], sibling[v, span(c)]
                outbox[0, v, span(c)] = combine(a, b, facing, down)
                outbox[1, v, span(c)] = combine(b, a, facing, up)
            to_link(outbox.at[1], c, 1).start()
            to_link(outbox.at[0], c, 0).start()

        pl.semaphore_wait(near_sem, 1)
        each(0, RAW, send_raw)
        each(RAW, CHUNKS, send_partial)

    @pl.when(second)
    def _():
        each(0, face_chunk, lambda c: to_sibling(c).wait_recv())
        got_front.wait()

    got_jac.wait()
    got_src.wait()

    def base(c):
        here = span(c)
        half_groups = pl.ds(c * (GROUP // 2), GROUP // 2)
        state = [own[w, here] for w in range(NV)]
        for v in range(NV):
            flux = 0.0
            for w in range(NV):
                block = jac[w, v, half_groups].astype(jnp.float32).reshape(GROUP, 8, LANES)
                flux = flux + block * state[w]
            coupled = combine(state[v], sibling[v, here], inner, near)
            result[v, here] = state[v] + coupled - pseudo_step * (flux - src[v, here])

    each(0, CHUNKS, base)
    each(0, face_groups, locate)

    @pl.when(second)
    def _():
        each(1, OWNERS, lambda k: scatter(k).wait_recv())
        sum_here = part[me]
        for k in range(1, OWNERS):
            sum_here = sum_here + gathered[k]
        half_sum[...] = sum_here
        across.start()
        across.wait_recv()
        total[...] = half_sum[...] + other_sum[...]
        for k in FAR_FIRST:
            gather(k).start()

        @pl.when(y >= 2)
        def _():
            gather(0).start()

        @pl.when(y < 2)
        def _():
            keep().start()

    def pass_on(c):
        to_link(inbox, c, 0).wait_recv()
        to_relay(c).start()

    each(0, RAW, pass_on)

    def finish_raw(c):
        to_relay(c).wait()
        for v in range(NV):
            result[v, span(c)] += combine(inbox[v, span(c)], relay[v, span(c)], facing, away)

    each(0, RAW, finish_raw)

    def finish(c):
        to_link(inbox, c, 0).wait_recv()
        result[:, span(c)] += inbox[:, span(c)]

    each(RAW, face_chunk, finish)

    odd_wide = lax.broadcasted_iota(jnp.int32, (8, BANDS), 0) % 2 == 1
    each(0, OWNERS // 2, lambda n: arrived(n).wait_recv())
    for h in range(2):
        sums = 0.0
        for p in range(PLANES):
            sums += jnp.concatenate([means[2 * p], means[2 * p + 1]], axis=1) * on_plane[h][p]
        total_area = sums[2 * NV : 2 * NV + 1]
        mean = sums / jnp.where(total_area > 0, total_area, 1.0)
        mean = mean * (pseudo_step * coupling_gain)
        by_row = [
            jnp.where(odd_wide, mean[2 * v + 1 : 2 * v + 2], mean[2 * v : 2 * v + 1]) for v in range(NV)
        ]

        def mix(n):
            g = h * (face_groups // 2) + n
            here = face_start + g
            band = index[g]
            lane = band % LANES
            for v in range(NV):
                face_mean = jnp.where(
                    band < LANES,
                    jnp.take_along_axis(by_row[v][:, :LANES], lane, axis=1, mode="promise_in_bounds"),
                    jnp.take_along_axis(by_row[v][:, LANES:], lane, axis=1, mode="promise_in_bounds"),
                )
                result[v, here] += own[v, here] * (pseudo_step * coupling_gain) - face_mean

        each(0, face_groups // 2, mix)

    each(face_chunk, CHUNKS, finish)

    each(0, CHUNKS, lambda c: to_sibling(c).wait_send())

    @pl.when(first)
    def _():
        each(0, CHUNKS, lambda c: to_link(inbox, c, 0).wait_send())
        each(0, CHUNKS, lambda c: to_link(inbox, c, 1).wait_send())

    @pl.when(second)
    def _():
        each(1, OWNERS, lambda k: scatter(k).wait_send())
        across.wait_send()
        each(1, OWNERS, lambda k: gather(k).wait_send())

        @pl.when(y >= 2)
        def _():
            gather(0).wait_send()


def hbm(x):
    return pltpu.with_memory_space_constraint(x, pltpu.HBM)


def fold(x):
    cells = x.shape[2]
    x = x.reshape(2, NV, cells // (4 * LANES), 4, LANES).transpose(1, 2, 3, 0, 4)
    return x.reshape(NV, cells // (4 * LANES), 8, LANES)


def unfold(x):
    x = x.reshape(NV, x.shape[1], 4, 2, LANES).transpose(3, 0, 1, 2, 4)
    return x.reshape(2, NV, -1)


def fold_jacobian(x):
    cells = x.shape[3]
    x = x.reshape(2, NV, NV, cells // (8 * LANES), 8, LANES).transpose(1, 2, 3, 4, 0, 5)
    return x.reshape(NV, NV, cells // (8 * LANES), 16, LANES)


def shards(adjoint, jacobian, source_term, face_area, face_band, partition_row):
    cells, faces = adjoint.shape[2], face_area.shape[0]
    groups = cells // (4 * LANES)
    assert groups == GROUP * CHUNKS
    f32, bf16, i32 = jnp.float32, jnp.bfloat16, jnp.int32
    dma = pltpu.SemaphoreType.DMA
    state = pltpu.VMEM((NV, groups, 8, LANES), f32)
    box = pltpu.VMEM((16, LANES), f32)
    boxes = pltpu.VMEM((OWNERS, 16, LANES), f32)
    updated = pl.pallas_call(
        kernel,
        out_shape=pltpu.VMEM((NV, groups, 8, LANES), f32),
        in_specs=[pl.BlockSpec(memory_space=pl.ANY)] * 5 + [pl.BlockSpec(memory_space=pltpu.SMEM)],
        out_specs=pl.BlockSpec(memory_space=pltpu.VMEM),
        scratch_shapes=[
            state,
            pltpu.VMEM((NV, NV, groups // 2, 16, LANES), bf16),
            state,
            state,
            pltpu.VMEM((2, NV, groups, 8, LANES), f32),
            state,
            pltpu.VMEM((NV, RAW * GROUP, 8, LANES), f32),
            pltpu.VMEM((faces // LANES, LANES), f32),
            pltpu.VMEM((faces // LANES, LANES), i32),
            pltpu.VMEM((BANDS, faces), bf16),
            pltpu.VMEM((faces // (4 * LANES), 8, LANES), i32),
            pltpu.VMEM((32, faces), f32),
            boxes,
            boxes,
            box,
            box,
            box,
            pltpu.VMEM((OWNERS // 2, 16, LANES), f32),
            pltpu.SemaphoreType.REGULAR,
            dma((6,)),
            dma((CHUNKS,)),
            dma((CHUNKS,)),
            dma((2, CHUNKS)),
            dma((CHUNKS,)),
            dma((RAW,)),
            dma((RAW,)),
            dma((OWNERS,)),
            dma((OWNERS,)),
            dma,
            dma,
            dma((OWNERS,)),
            dma((OWNERS // 2,)),
        ],
        compiler_params=pltpu.CompilerParams(
            collective_id=0, has_side_effects=True, vmem_limit_bytes=40 << 20
        ),
    )(
        hbm(fold(adjoint)),
        hbm(fold_jacobian(jacobian)),
        hbm(fold(source_term)),
        hbm(face_area.reshape(faces // LANES, LANES)),
        hbm(face_band.reshape(faces // LANES, LANES)),
        partition_row,
    )
    return unfold(updated)


def solution(mesh):
    placed = (
        P("inst", None, "rows"),
        P("inst", None, None, "rows"),
        P("inst", None, "rows"),
        P("rows"),
        P("rows"),
        P("rows"),
    )
    return jax.shard_map(
        shards, mesh=mesh, in_specs=placed, out_specs=P("inst", None, "rows"), check_vma=False
    )
```

```python
import jax
import jax.numpy as jnp
import numpy as np
from jax import lax
from jax.experimental import pallas as pl
from jax.experimental.pallas import tpu as pltpu
from jax.sharding import PartitionSpec as P

MESH = pl.DeviceIdType.MESH
NT = 8
NV = 5
NB = 200
PLANES = 4
BANDS = 256
LANES = 128

frequency = 1.0
coupling_gain = 2.0
pseudo_step = 0.5

SENDER = 0
GROUPS = 36
RAW = 8
PARTS = 4
PART = (GROUPS - RAW) // PARTS
OWNERS = 16


def ring(k):
    return min(k, 4 - k)


FAR_FIRST = sorted(range(1, OWNERS), key=lambda k: -ring(k // 4) - ring(k % 4))


def spectral(offset):
    if offset % NT == 0:
        return 0.0
    angle = np.float32(np.pi * offset / NT)
    return float(np.float32(0.5 * (-1) ** (offset % 2)) / np.tan(angle))


def weight_of(offset):
    return -pseudo_step * frequency * spectral(offset)


def pick(first, up, down):
    return jnp.where(first, jnp.float32(up), jnp.float32(down))


def swap(x):
    even = lax.broadcasted_iota(jnp.int32, x.shape, x.ndim - 2) % 2 == 0
    return jnp.where(even, pltpu.roll(x, 7, x.ndim - 2), pltpu.roll(x, 1, x.ndim - 2))


def split(x):
    high = x.astype(jnp.bfloat16)
    low = (x - high.astype(jnp.float32)).astype(jnp.bfloat16)
    return jnp.concatenate([high, low], axis=0)


def kernel(
    adjoint, jacobian, source, area, band, owner, result,
    own, jac, src, sibling, outbox, inbox, raw, relay, area_v, band_v,
    table, index, weighted, part, gathered, half_sum, other_sum, total, means,
    near_sem, local_sem, sib_send, sib_recv, raw_send, raw_recv, link_send, link_recv, relay_send, relay_recv,
    rs_send, rs_recv, x_send, x_recv, ag_send, ag_recv,
):
    rows, inst = lax.axis_index("rows"), lax.axis_index("inst")
    z, x_hi, y = rows // 8, (rows // 4) % 2, rows % 4
    core = inst % 2
    sender, agent = core == SENDER, core != SENDER
    sibling_id = (rows, inst + 1 - 2 * core)
    link_id = (rows, (inst + 2) % 4)
    across_id = (z * 8 + (1 - x_hi) * 4 + y, inst)
    me = z * 4 + y
    faces = weighted.shape[1]
    half = faces // 2
    face_groups = faces // (4 * LANES)
    face_start = GROUPS - face_groups
    cuts = ((face_start, GROUPS), (0, face_start)), ((0, RAW), (RAW, RAW + PART), (RAW + PART, GROUPS))

    def place(k):
        return (z + k // 4) % 4, (y + k % 4) % 4

    def device(k, inst):
        zd, yd = place(k)
        return (zd * 8 + x_hi * 4 + yd, inst)

    def span(n):
        return pl.ds(RAW + n * PART, PART)

    def each(low, high, act):
        def body(k, carry):
            act(k)
            return carry

        lax.fori_loop(low, high, body, 0)

    def fetch(k, a, b):
        copy = pltpu.make_async_copy(a, b, local_sem.at[k])
        copy.start()
        return copy

    def drain(like, sem):
        pltpu.make_async_copy(like, like, sem).wait()

    def signal(sem, device_id):
        pl.semaphore_signal(sem, inc=1, device_id=device_id, device_id_type=MESH)

    def remote(a, b, send, recv, device_id):
        return pltpu.make_async_remote_copy(
            a, b, send, recv, device_id=device_id, device_id_type=MESH
        )

    def give(pieces):
        for n, (low, high) in enumerate(pieces):
            here = pl.ds(low, high - low)
            remote(adjoint.at[:, here], sibling.at[:, here], sib_send, sib_recv.at[n], sibling_id).start()

    def given(pieces, n):
        low, high = pieces[n]
        drain(sibling.at[:, pl.ds(low, high - low)], sib_recv.at[n])

    def beyond(other):
        return (rows, (inst + 2) % 4 + other * (1 - 2 * core))

    def raw_to_link(given, other):
        here = given.at[:, pl.ds(0, RAW)]
        return remote(here, raw, raw_send.at[other], raw_recv, beyond(other))

    def to_link(n, other):
        arrival = link_recv.at[n // (PARTS - 1)]
        return remote(outbox.at[other, n], inbox.at[n], link_send, arrival, beyond(other))

    def to_relay():
        return remote(raw, relay, relay_send, relay_recv, sibling_id)

    def scatter(k):
        zd, yd = place(k)
        return remote(part.at[zd * 4 + yd], gathered.at[k], rs_send, rs_recv, device(k, inst))

    slot = 2 * z + y % 2
    served = inst + (y // 2) * (1 - 2 * core)

    def gather(k):
        return remote(total, means.at[slot], ag_send, ag_recv, device(k, served))

    def keep():
        return pltpu.make_async_copy(total, means.at[slot], ag_recv)

    across = remote(half_sum, other_sum, x_send, x_recv, across_id)

    barrier = pltpu.get_barrier_semaphore()

    @pl.when(sender)
    def _():
        signal(barrier, link_id)

    @pl.when(agent)
    def _():
        signal(barrier, sibling_id)
        for k in FAR_FIRST:
            signal(barrier, device(k, inst))
        signal(barrier, across_id)

    tail, front = pl.ds(face_start, face_groups), pl.ds(0, face_start)
    got_faces = fetch(0, adjoint.at[:, tail], own.at[:, tail])
    got_area = fetch(1, area, area_v)
    got_band = fetch(2, band, band_v)
    got_front = fetch(3, adjoint.at[:, front], own.at[:, front])
    got_jac = fetch(4, jacobian, jac)
    got_src = fetch(5, source, src)

    @pl.when(sender)
    def _():
        pl.semaphore_wait(barrier, 2)
        signal(near_sem, sibling_id)
        signal(near_sem, link_id)
        raw_to_link(adjoint, 0).start()
        give(cuts[0])

    @pl.when(agent)
    def _():
        pl.semaphore_wait(near_sem, 1)
        give(cuts[1])

    got_area.wait()
    got_band.wait()
    band_index = lax.broadcasted_iota(jnp.int32, (BANDS, LANES), 0)
    block_row = lax.broadcasted_iota(jnp.int32, (8, LANES), 0)

    def locate(g):
        bands = band_v[pl.ds(4 * g, 1), :]
        for r in range(1, 4):
            bands = jnp.where(block_row < 2 * r, bands, band_v[pl.ds(4 * g + r, 1), :])
        index[g] = bands

    def mark(n):
        here = pl.ds(pl.multiple_of(n * LANES, LANES), LANES)
        table[:, here] = jnp.where(band_index == band_v[pl.ds(n, 1), :], 1.0, 0.0).astype(jnp.bfloat16)

    row = owner[0]
    planes = (jnp.maximum(row - 1, 0), jnp.minimum(row, PLANES - 1))
    on_plane = [
        [jnp.where(planes[h] == p, jnp.float32(1), jnp.float32(0)) for p in range(PLANES)]
        for h in range(2)
    ]

    def weigh(values, top):
        def group(g):
            for r in range(4):
                tile = 4 * g + r
                here = pl.ds(pl.multiple_of(tile * LANES, LANES), LANES)
                size = area_v[pl.ds(tile, 1), :]
                for v in range(NV):
                    weighted[top + 2 * v : top + 2 * v + 2, here] = (
                        values[v, face_start + g, 2 * r : 2 * r + 2, :] * size
                    )
                weighted[top + 2 * NV : top + 2 * NV + 1, here] = size

        each(0, face_groups, group)

    @pl.when(agent)
    def _():
        each(0, faces // LANES, mark)
        weighted[...] = jnp.zeros_like(weighted)
        got_faces.wait()
        weigh(own, 0)
        given(cuts[0], 0)
        weigh(sibling, 16)
        sums = []
        for h in range(2):
            cut = slice(h * half, (h + 1) * half)
            both = lax.dot_general(
                split(weighted[:, cut]), table[:, cut], (((1,), (1,)), ((), ())),
                preferred_element_type=jnp.float32,
            )
            sums.append(both[0:32] + both[32:64])
        for p in range(PLANES):
            here = sums[0] * on_plane[0][p] + sums[1] * on_plane[1][p]
            for q in range(4):
                part[4 * p + q] = here[
                    16 * (q // 2) : 16 * (q // 2) + 16, LANES * (q % 2) : LANES * (q % 2 + 1)
                ]
        pl.semaphore_wait(barrier, OWNERS)
        for k in FAR_FIRST:
            scatter(k).start()

    odd = block_row % 2 == 1

    def weights(by_offset):
        return by_offset[0], jnp.where(odd, by_offset[1], by_offset[-1])

    shifts = (-1, 0, 1)
    inner = weights({d: weight_of(d) for d in shifts})
    facing = weights({d: weight_of(4 + d) for d in shifts})
    skew = 2 if SENDER else -2
    for_facing = weights({d: weight_of(skew + d) for d in shifts})
    for_other = weights({d: weight_of(-skew + d) for d in shifts})
    near = weights({d: pick(core == 0, weight_of(2 + d), weight_of(-2 + d)) for d in shifts})
    away = weights({d: pick(core == 0, weight_of(-2 + d), weight_of(2 + d)) for d in shifts})

    def combine(a, b, wa, wb):
        return wa[0] * a + wb[0] * b + swap(wa[1] * a + wb[1] * b)

    @pl.when(sender)
    def _():
        pl.semaphore_wait(near_sem, 1)
        given(cuts[1], 0)
        raw_to_link(sibling, 1).start()
        got_front.wait()
        got_faces.wait()
        for n in range(PARTS):
            if n < 2:
                given(cuts[1], n + 1)

            def mix_instances(v):
                a, b = own[v, span(n)], sibling[v, span(n)]
                outbox[1, n, v] = combine(b, a, facing, for_other)
                outbox[0, n, v] = combine(a, b, facing, for_facing)

            each(0, NV, mix_instances)
            to_link(n, 1).start()
            to_link(n, 0).start()

    @pl.when(agent)
    def _():
        given(cuts[0], 1)
        got_front.wait()

    got_jac.wait()
    got_src.wait()

    def base(m):
        here = pl.ds(4 * m, 4)
        state = [own[w, here] for w in range(NV)]
        for v in range(NV):
            flux = 0.0
            for w in range(NV):
                block = jac[w, v, pl.ds(2 * m, 2)].astype(jnp.float32).reshape(4, 8, LANES)
                flux = flux + block * state[w]
            coupled = combine(state[v], sibling[v, here], inner, near)
            result[v, here] = state[v] + coupled - pseudo_step * (flux - src[v, here])

    each(0, GROUPS // 4, base)
    each(0, face_groups, locate)

    @pl.when(agent)
    def _():
        drain(gathered.at[pl.ds(1, OWNERS - 1)], rs_recv)
        sum_here = part[me]
        for k in range(1, OWNERS):
            sum_here = sum_here + gathered[k]
        half_sum[...] = sum_here
        across.start()
        across.wait_recv()
        total[...] = half_sum[...] + other_sum[...]
        for k in FAR_FIRST:
            gather(k).start()

        @pl.when(y >= 2)
        def _():
            gather(0).start()

        @pl.when(y < 2)
        def _():
            keep().start()

    raw_to_link(adjoint, 0).wait_recv()
    to_relay().start()

    def finish(n):
        result[:, span(n)] += inbox[n]

    drain(inbox.at[pl.ds(0, PARTS - 1)], link_recv.at[0])
    each(0, PARTS - 1, finish)

    to_relay().wait()
    for v in range(NV):
        result[v, 0:RAW] += combine(raw[v], relay[v], facing, away)

    odd_wide = lax.broadcasted_iota(jnp.int32, (8, BANDS), 0) % 2 == 1
    drain(means, ag_recv)
    for h in range(2):
        sums = 0.0
        for p in range(PLANES):
            sums += jnp.concatenate([means[2 * p], means[2 * p + 1]], axis=1) * on_plane[h][p]
        total_area = sums[2 * NV : 2 * NV + 1]
        mean = sums / jnp.where(total_area > 0, total_area, 1.0)
        mean = mean * (pseudo_step * coupling_gain)
        by_row = [
            jnp.where(odd_wide, mean[2 * v + 1 : 2 * v + 2], mean[2 * v : 2 * v + 1]) for v in range(NV)
        ]

        def mix(n):
            g = h * (face_groups // 2) + n
            here = face_start + g
            band = index[g]
            lane = band % LANES
            for v in range(NV):
                face_mean = jnp.where(
                    band < LANES,
                    jnp.take_along_axis(by_row[v][:, :LANES], lane, axis=1, mode="promise_in_bounds"),
                    jnp.take_along_axis(by_row[v][:, LANES:], lane, axis=1, mode="promise_in_bounds"),
                )
                result[v, here] += own[v, here] * (pseudo_step * coupling_gain) - face_mean

        each(0, face_groups // 2, mix)

    drain(inbox.at[PARTS - 1], link_recv.at[1])
    finish(PARTS - 1)

    drain(sibling, sib_send)

    @pl.when(sender)
    def _():
        for other in range(2):
            raw_to_link(adjoint, other).wait_send()
        drain(outbox, link_send)

    @pl.when(agent)
    def _():
        across.wait_send()
        drain(gathered.at[pl.ds(1, OWNERS - 1)], rs_send)

        @pl.when(y >= 2)
        def _():
            drain(gathered, ag_send)

        @pl.when(y < 2)
        def _():
            drain(gathered.at[pl.ds(1, OWNERS - 1)], ag_send)


def hbm(x):
    return pltpu.with_memory_space_constraint(x, pltpu.HBM)


def fold(x):
    cells = x.shape[2]
    x = x.reshape(2, NV, cells // (4 * LANES), 4, LANES).transpose(1, 2, 3, 0, 4)
    return x.reshape(NV, cells // (4 * LANES), 8, LANES)


def unfold(x):
    x = x.reshape(NV, x.shape[1], 4, 2, LANES).transpose(3, 0, 1, 2, 4)
    return x.reshape(2, NV, -1)


def fold_jacobian(x):
    cells = x.shape[3]
    x = x.reshape(2, NV, NV, cells // (8 * LANES), 8, LANES).transpose(1, 2, 3, 4, 0, 5)
    return x.reshape(NV, NV, cells // (8 * LANES), 16, LANES)


def shards(adjoint, jacobian, source_term, face_area, face_band, partition_row):
    cells, faces = adjoint.shape[2], face_area.shape[0]
    groups = cells // (4 * LANES)
    assert groups == GROUPS
    f32, bf16, i32 = jnp.float32, jnp.bfloat16, jnp.int32
    dma = pltpu.SemaphoreType.DMA
    state = pltpu.VMEM((NV, groups, 8, LANES), f32)
    box = pltpu.VMEM((16, LANES), f32)
    boxes = pltpu.VMEM((OWNERS, 16, LANES), f32)
    updated = pl.pallas_call(
        kernel,
        out_shape=pltpu.VMEM((NV, groups, 8, LANES), f32),
        in_specs=[pl.BlockSpec(memory_space=pl.ANY)] * 5 + [pl.BlockSpec(memory_space=pltpu.SMEM)],
        out_specs=pl.BlockSpec(memory_space=pltpu.VMEM),
        scratch_shapes=[
            state,
            pltpu.VMEM((NV, NV, groups // 2, 16, LANES), bf16),
            state,
            state,
            pltpu.VMEM((2, PARTS, NV, PART, 8, LANES), f32),
            pltpu.VMEM((PARTS, NV, PART, 8, LANES), f32),
            pltpu.VMEM((NV, RAW, 8, LANES), f32),
            pltpu.VMEM((NV, RAW, 8, LANES), f32),
            pltpu.VMEM((faces // LANES, LANES), f32),
            pltpu.VMEM((faces // LANES, LANES), i32),
            pltpu.VMEM((BANDS, faces), bf16),
            pltpu.VMEM((faces // (4 * LANES), 8, LANES), i32),
            pltpu.VMEM((32, faces), f32),
            boxes,
            boxes,
            box,
            box,
            box,
            pltpu.VMEM((OWNERS // 2, 16, LANES), f32),
            pltpu.SemaphoreType.REGULAR,
            dma((6,)),
            dma,
            dma((3,)),
            dma((2,)),
            dma,
            dma,
            dma((2,)),
            dma,
            dma,
            dma,
            dma,
            dma,
            dma,
            dma,
            dma,
        ],
        compiler_params=pltpu.CompilerParams(
            collective_id=0, has_side_effects=True, vmem_limit_bytes=40 << 20
        ),
    )(
        hbm(fold(adjoint)),
        hbm(fold_jacobian(jacobian)),
        hbm(fold(source_term)),
        hbm(face_area.reshape(faces // LANES, LANES)),
        hbm(face_band.reshape(faces // LANES, LANES)),
        partition_row,
    )
    return unfold(updated)


def solution(mesh):
    placed = (
        P("inst", None, "rows"),
        P("inst", None, None, "rows"),
        P("inst", None, "rows"),
        P("rows"),
        P("rows"),
        P("rows"),
    )
    return jax.shard_map(
        shards, mesh=mesh, in_specs=placed, out_specs=P("inst", None, "rows"), check_vma=False
    )
```

```python
import jax
import jax.numpy as jnp
import numpy as np
from jax import lax
from jax.experimental import pallas as pl
from jax.experimental.pallas import tpu as pltpu
from jax.sharding import PartitionSpec as P

MESH = pl.DeviceIdType.MESH
NT = 8
NV = 5
NB = 200
PLANES = 4
BANDS = 256
LANES = 128

frequency = 1.0
coupling_gain = 2.0
pseudo_step = 0.5

SENDER = 0
GROUPS = 36
RAW = 8
PARTS = 4
PART = (GROUPS - RAW) // PARTS
OWNERS = 16


def ring(k):
    return min(k, 4 - k)


FAR_FIRST = sorted(range(1, OWNERS), key=lambda k: -ring(k // 4) - ring(k % 4))


def spectral(offset):
    if offset % NT == 0:
        return 0.0
    angle = np.float32(np.pi * offset / NT)
    return float(np.float32(0.5 * (-1) ** (offset % 2)) / np.tan(angle))


def weight_of(offset):
    return -pseudo_step * frequency * spectral(offset)


def pick(first, up, down):
    return jnp.where(first, jnp.float32(up), jnp.float32(down))


def swap(x):
    even = lax.broadcasted_iota(jnp.int32, x.shape, x.ndim - 2) % 2 == 0
    return jnp.where(even, pltpu.roll(x, 7, x.ndim - 2), pltpu.roll(x, 1, x.ndim - 2))


def split(x):
    high = x.astype(jnp.bfloat16)
    low = (x - high.astype(jnp.float32)).astype(jnp.bfloat16)
    return jnp.concatenate([high, low], axis=0)


def kernel(
    adjoint, jacobian, source, area, band, owner, result,
    own, jac, src, sibling, outbox, inbox, raw, relay, area_v, band_v,
    table, index, weighted, part, gathered, half_sum, other_sum, total, means,
    near_sem, local_sem, sib_send, sib_recv, raw_send, raw_recv, link_send, link_recv, relay_send, relay_recv,
    rs_send, rs_recv, x_send, x_recv, ag_send, ag_recv,
):
    rows, inst = lax.axis_index("rows"), lax.axis_index("inst")
    z, x_hi, y = rows // 8, (rows // 4) % 2, rows % 4
    core = inst % 2
    sender, agent = core == SENDER, core != SENDER
    sibling_id = (rows, inst + 1 - 2 * core)
    link_id = (rows, (inst + 2) % 4)
    across_id = (z * 8 + (1 - x_hi) * 4 + y, inst)
    me = z * 4 + y
    faces = weighted.shape[1]
    half = faces // 2
    face_groups = faces // (4 * LANES)
    face_start = GROUPS - face_groups
    face_middle = face_start + face_groups // 2
    cuts = (
        ((face_start, face_middle), (face_middle, GROUPS), (0, face_start)),
        ((0, RAW), (RAW, RAW + PART), (RAW + PART, GROUPS)),
    )

    def place(k):
        return (z + k // 4) % 4, (y + k % 4) % 4

    def device(k, inst):
        zd, yd = place(k)
        return (zd * 8 + x_hi * 4 + yd, inst)

    def span(n):
        return pl.ds(RAW + n * PART, PART)

    def each(low, high, act):
        def body(k, carry):
            act(k)
            return carry

        lax.fori_loop(low, high, body, 0)

    def fetch(k, a, b):
        return pltpu.make_async_copy(a, b, local_sem.at[k])

    def drain(like, sem):
        pltpu.make_async_copy(like, like, sem).wait()

    def signal(sem, device_id):
        pl.semaphore_signal(sem, inc=1, device_id=device_id, device_id_type=MESH)

    def remote(a, b, send, recv, device_id):
        return pltpu.make_async_remote_copy(
            a, b, send, recv, device_id=device_id, device_id_type=MESH
        )

    def give(pieces):
        for n, (low, high) in enumerate(pieces):
            here = pl.ds(low, high - low)
            remote(adjoint.at[:, here], sibling.at[:, here], sib_send, sib_recv.at[n], sibling_id).start()

    def given(pieces, n):
        low, high = pieces[n]
        drain(sibling.at[:, pl.ds(low, high - low)], sib_recv.at[n])

    def beyond(other):
        return (rows, (inst + 2) % 4 + other * (1 - 2 * core))

    def raw_to_link(state, other):
        here = state.at[:, pl.ds(0, RAW)]
        return remote(here, raw, raw_send.at[other], raw_recv, beyond(other))

    def to_link(n, other):
        arrival = link_recv.at[n // (PARTS - 1)]
        return remote(outbox.at[other * PARTS + n], inbox.at[n], link_send, arrival, beyond(other))

    def to_relay():
        return remote(raw, relay, relay_send, relay_recv, sibling_id)

    def scatter(k):
        zd, yd = place(k)
        return remote(part.at[zd * 4 + yd], gathered.at[k], rs_send, rs_recv, device(k, inst))

    slot = 2 * z + y % 2
    served = inst + (y // 2) * (1 - 2 * core)

    def gather(k):
        return remote(total, means.at[slot], ag_send, ag_recv, device(k, served))

    def keep():
        return pltpu.make_async_copy(total, means.at[slot], ag_recv)

    across = remote(half_sum, other_sum, x_send, x_recv, across_id)

    barrier = pltpu.get_barrier_semaphore()

    @pl.when(sender)
    def _():
        signal(barrier, link_id)

    @pl.when(agent)
    def _():
        signal(barrier, sibling_id)
        for k in FAR_FIRST:
            signal(barrier, device(k, inst))
        signal(barrier, across_id)

    head, middle, tail = pl.ds(0, RAW), pl.ds(RAW, face_start - RAW), pl.ds(face_start, face_groups)
    got_head = fetch(0, adjoint.at[:, head], own.at[:, head])
    got_middle = fetch(1, adjoint.at[:, middle], own.at[:, middle])
    got_faces = fetch(2, adjoint.at[:, tail], own.at[:, tail])
    got_area = fetch(3, area, area_v)
    got_band = fetch(4, band, band_v)
    got_jac = fetch(5, jacobian, jac)
    got_src = fetch(6, source, src)

    @pl.when(sender)
    def _():
        got_head.start()
        got_middle.start()
        got_faces.start()
        pl.semaphore_wait(barrier, 2)
        signal(near_sem, sibling_id)
        signal(near_sem, link_id)
        raw_to_link(adjoint, 0).start()
        give(cuts[0])
        got_band.start()
        got_jac.start()
        got_src.start()

    @pl.when(agent)
    def _():
        got_band.start()
        got_faces.start()
        got_area.start()
        got_head.start()
        got_middle.start()
        got_jac.start()
        got_src.start()
        pl.semaphore_wait(near_sem, 1)
        give(cuts[1])

    block_row = lax.broadcasted_iota(jnp.int32, (8, LANES), 0)

    def locate(g):
        bands = band_v[pl.ds(4 * g, 1), :]
        for r in range(1, 4):
            bands = jnp.where(block_row < 2 * r, bands, band_v[pl.ds(4 * g + r, 1), :])
        index[g] = bands

    row = owner[0]
    planes = (jnp.maximum(row - 1, 0), jnp.minimum(row, PLANES - 1))
    on_plane = [
        [jnp.where(planes[h] == p, jnp.float32(1), jnp.float32(0)) for p in range(PLANES)]
        for h in range(2)
    ]

    def turned(x, by):
        return x if by % 8 == 0 else pltpu.roll(x, by % 8, 0)

    def weigh(values, top, low, high):
        def group(g):
            blocks = [values[v, face_start + g] for v in range(4)]
            for r in range(4):
                here = pl.ds(pl.multiple_of((4 * g + r) * LANES, LANES), LANES)
                rows = turned(blocks[0], -2 * r)
                for v in range(1, 4):
                    rows = jnp.where(block_row // 2 == v, turned(blocks[v], 2 * v - 2 * r), rows)
                weighted[top : top + 8, here] = rows * area_v[pl.ds(4 * g + r, 1), :]

        each(low, high, group)

    def weigh_last(low, high):
        def group(g):
            mine, other = own[NV - 1, face_start + g], sibling[NV - 1, face_start + g]
            for r in range(4):
                here = pl.ds(pl.multiple_of((4 * g + r) * LANES, LANES), LANES)
                rows = jnp.where(block_row < 2, turned(mine, -2 * r), turned(other, 2 - 2 * r))
                rows = jnp.where(block_row < 4, rows, jnp.where(block_row == 4, 1.0, 0.0))
                weighted[16:24, here] = rows * area_v[pl.ds(4 * g + r, 1), :]

        each(low, high, group)

    @pl.when(agent)
    def _():
        got_band.wait()
        band_lane = lax.broadcasted_iota(jnp.int32, (LANES, BANDS), 1)
        by_face = jnp.transpose(band_v[...])
        for n in range(faces // LANES):
            here = jnp.where(band_lane == by_face[:, n : n + 1], 1.0, 0.0)
            table[n * LANES : (n + 1) * LANES, :] = here.astype(jnp.bfloat16)
        got_area.wait()
        got_faces.wait()
        weigh(own, 0, 0, face_groups)
        sums = []
        for h in range(2):
            given(cuts[0], h)
            low, high = h * (face_groups // 2), (h + 1) * (face_groups // 2)
            weigh(sibling, 8, low, high)
            weigh_last(low, high)
            cut = slice(h * half, (h + 1) * half)
            both = jnp.dot(split(weighted[:, cut]), table[cut, :], preferred_element_type=jnp.float32)
            sums.append(both[0:24] + both[24:48])
        for p in range(PLANES):
            here = sums[0] * on_plane[0][p] + sums[1] * on_plane[1][p]
            for q in range(4):
                cut = slice(LANES * (q % 2), LANES * (q % 2 + 1))
                part[4 * p + q, 0:8] = here[8 * (q // 2) : 8 * (q // 2) + 8, cut]
                part[4 * p + q, 8:16] = here[16:24, cut]
        pl.semaphore_wait(barrier, OWNERS)
        for k in FAR_FIRST:
            scatter(k).start()

    odd = block_row % 2 == 1

    def weights(by_offset):
        return by_offset[0], jnp.where(odd, by_offset[1], by_offset[-1])

    shifts = (-1, 0, 1)
    inner = weights({d: weight_of(d) for d in shifts})
    facing = weights({d: weight_of(4 + d) for d in shifts})
    skew = 2 if SENDER else -2
    for_facing = weights({d: weight_of(skew + d) for d in shifts})
    for_other = weights({d: weight_of(-skew + d) for d in shifts})
    near = weights({d: pick(core == 0, weight_of(2 + d), weight_of(-2 + d)) for d in shifts})
    away = weights({d: pick(core == 0, weight_of(-2 + d), weight_of(2 + d)) for d in shifts})

    def combine(a, b, wa, wb):
        return wa[0] * a + wb[0] * b + swap(wa[1] * a + wb[1] * b)

    @pl.when(sender)
    def _():
        pl.semaphore_wait(near_sem, 1)
        given(cuts[1], 0)
        raw_to_link(sibling, 1).start()
        got_head.wait()
        got_middle.wait()
        got_faces.wait()
        for n in range(PARTS):
            if n < 2:
                given(cuts[1], n + 1)

            def mix_instances(v):
                a, b = own[v, span(n)], sibling[v, span(n)]
                outbox[PARTS + n, v] = combine(b, a, facing, for_other)
                outbox[n, v] = combine(a, b, facing, for_facing)

            each(0, NV, mix_instances)
            to_link(n, 1).start()
            to_link(n, 0).start()
        got_band.wait()

    def base(m):
        here = pl.ds(4 * m, 4)
        state = [own[w, here] for w in range(NV)]
        for v in range(NV):
            flux = 0.0
            for w in range(NV):
                block = jac[w, v, pl.ds(2 * m, 2)].astype(jnp.float32).reshape(4, 8, LANES)
                flux = flux + block * state[w]
            coupled = combine(state[v], sibling[v, here], inner, near)
            result[v, here] = state[v] + coupled - pseudo_step * (flux - src[v, here])

    def bases():
        got_jac.wait()
        got_src.wait()
        each(0, GROUPS // 4, base)
        each(0, face_groups, locate)

    @pl.when(sender)
    def _():
        bases()

    @pl.when(agent)
    def _():
        drain(gathered.at[pl.ds(1, OWNERS - 1)], rs_recv)
        sum_here = part[me]
        for k in range(1, OWNERS):
            sum_here = sum_here + gathered[k]
        half_sum[...] = sum_here
        across.start()
        given(cuts[0], 2)
        got_head.wait()
        got_middle.wait()
        bases()
        across.wait_recv()
        total[...] = half_sum[...] + other_sum[...]
        for k in FAR_FIRST:
            gather(k).start()

        @pl.when(y >= 2)
        def _():
            gather(0).start()

        @pl.when(y < 2)
        def _():
            keep().start()

    raw_to_link(adjoint, 0).wait_recv()
    to_relay().start()

    def finish(n):
        result[:, span(n)] += inbox[n]

    drain(inbox.at[pl.ds(0, PARTS - 1)], link_recv.at[0])
    each(0, PARTS - 1, finish)

    to_relay().wait()
    for v in range(NV):
        result[v, 0:RAW] += combine(raw[v], relay[v], facing, away)

    odd_wide = lax.broadcasted_iota(jnp.int32, (8, BANDS), 0) % 2 == 1
    drain(means, ag_recv)
    for h in range(2):
        sums = 0.0
        for p in range(PLANES):
            sums += jnp.concatenate([means[2 * p], means[2 * p + 1]], axis=1) * on_plane[h][p]
        total_area = sums[12:13]
        mean = sums / jnp.where(total_area > 0, total_area, 1.0)
        mean = mean * (pseudo_step * coupling_gain)
        last = jnp.where(agent, mean[8:10], mean[10:12])
        by_row = [
            jnp.where(odd_wide, mean[2 * v + 1 : 2 * v + 2], mean[2 * v : 2 * v + 1]) for v in range(4)
        ] + [jnp.where(odd_wide, last[1:2], last[0:1])]

        def mix(n):
            g = h * (face_groups // 2) + n
            here = face_start + g
            band = index[g]
            lane = band % LANES
            for v in range(NV):
                face_mean = jnp.where(
                    band < LANES,
                    jnp.take_along_axis(by_row[v][:, :LANES], lane, axis=1, mode="promise_in_bounds"),
                    jnp.take_along_axis(by_row[v][:, LANES:], lane, axis=1, mode="promise_in_bounds"),
                )
                result[v, here] += own[v, here] * (pseudo_step * coupling_gain) - face_mean

        each(0, face_groups // 2, mix)

    drain(inbox.at[PARTS - 1], link_recv.at[1])
    finish(PARTS - 1)

    drain(sibling, sib_send)

    @pl.when(sender)
    def _():
        for other in range(2):
            raw_to_link(adjoint, other).wait_send()
        drain(outbox, link_send)

    @pl.when(agent)
    def _():
        across.wait_send()
        drain(gathered.at[pl.ds(1, OWNERS - 1)], rs_send)

        @pl.when(y >= 2)
        def _():
            drain(gathered, ag_send)

        @pl.when(y < 2)
        def _():
            drain(gathered.at[pl.ds(1, OWNERS - 1)], ag_send)


def hbm(x):
    return pltpu.with_memory_space_constraint(x, pltpu.HBM)


def fold(x):
    cells = x.shape[2]
    x = x.reshape(2, NV, cells // (4 * LANES), 4, LANES).transpose(1, 2, 3, 0, 4)
    return x.reshape(NV, cells // (4 * LANES), 8, LANES)


def unfold(x):
    x = x.reshape(NV, x.shape[1], 4, 2, LANES).transpose(3, 0, 1, 2, 4)
    return x.reshape(2, NV, -1)


def fold_jacobian(x):
    cells = x.shape[3]
    x = x.reshape(2, NV, NV, cells // (8 * LANES), 8, LANES).transpose(1, 2, 3, 4, 0, 5)
    return x.reshape(NV, NV, cells // (8 * LANES), 16, LANES)


def shards(adjoint, jacobian, source_term, face_area, face_band, partition_row):
    cells, faces = adjoint.shape[2], face_area.shape[0]
    groups = cells // (4 * LANES)
    assert groups == GROUPS
    f32, bf16, i32 = jnp.float32, jnp.bfloat16, jnp.int32
    dma = pltpu.SemaphoreType.DMA
    state = pltpu.VMEM((NV, groups, 8, LANES), f32)
    box = pltpu.VMEM((16, LANES), f32)
    boxes = pltpu.VMEM((OWNERS, 16, LANES), f32)
    updated = pl.pallas_call(
        kernel,
        out_shape=pltpu.VMEM((NV, groups, 8, LANES), f32),
        in_specs=[pl.BlockSpec(memory_space=pl.ANY)] * 5 + [pl.BlockSpec(memory_space=pltpu.SMEM)],
        out_specs=pl.BlockSpec(memory_space=pltpu.VMEM),
        scratch_shapes=[
            state,
            pltpu.VMEM((NV, NV, groups // 2, 16, LANES), bf16),
            state,
            state,
            pltpu.VMEM((2 * PARTS, NV, PART, 8, LANES), f32),
            pltpu.VMEM((PARTS, NV, PART, 8, LANES), f32),
            pltpu.VMEM((NV, RAW, 8, LANES), f32),
            pltpu.VMEM((NV, RAW, 8, LANES), f32),
            pltpu.VMEM((faces // LANES, LANES), f32),
            pltpu.VMEM((faces // LANES, LANES), i32),
            pltpu.VMEM((faces, BANDS), bf16),
            pltpu.VMEM((faces // (4 * LANES), 8, LANES), i32),
            pltpu.VMEM((24, faces), f32),
            boxes,
            boxes,
            box,
            box,
            box,
            pltpu.VMEM((OWNERS // 2, 16, LANES), f32),
            pltpu.SemaphoreType.REGULAR,
            dma((7,)),
            dma,
            dma((3,)),
            dma((2,)),
            dma,
            dma,
            dma((2,)),
            dma,
            dma,
            dma,
            dma,
            dma,
            dma,
            dma,
            dma,
        ],
        compiler_params=pltpu.CompilerParams(
            collective_id=0, has_side_effects=True, vmem_limit_bytes=40 << 20
        ),
    )(
        hbm(fold(adjoint)),
        hbm(fold_jacobian(jacobian)),
        hbm(fold(source_term)),
        hbm(face_area.reshape(faces // LANES, LANES)),
        hbm(face_band.reshape(faces // LANES, LANES)),
        partition_row,
    )
    return unfold(updated)


def solution(mesh):
    placed = (
        P("inst", None, "rows"),
        P("inst", None, None, "rows"),
        P("inst", None, "rows"),
        P("rows"),
        P("rows"),
        P("rows"),
    )
    return jax.shard_map(
        shards, mesh=mesh, in_specs=placed, out_specs=P("inst", None, "rows"), check_vma=False
    )
```

```python
import jax
import jax.numpy as jnp
import numpy as np
from jax import lax
from jax.experimental import pallas as pl
from jax.experimental.pallas import tpu as pltpu
from jax.sharding import PartitionSpec as P

MESH = pl.DeviceIdType.MESH
NT = 8
NV = 5
NB = 200
PLANES = 4
BANDS = 256
LANES = 128

frequency = 1.0
coupling_gain = 2.0
pseudo_step = 0.5

SENDER = 0
GROUPS = 36
RAW = 8
PARTS = 4
PART = (GROUPS - RAW) // PARTS
OWNERS = 16


def ring(k):
    return min(k, 4 - k)


FAR_FIRST = sorted(range(1, OWNERS), key=lambda k: -ring(k // 4) - ring(k % 4))


def spectral(offset):
    if offset % NT == 0:
        return 0.0
    angle = np.float32(np.pi * offset / NT)
    return float(np.float32(0.5 * (-1) ** (offset % 2)) / np.tan(angle))


def weight_of(offset):
    return -pseudo_step * frequency * spectral(offset)


def pick(first, up, down):
    return jnp.where(first, jnp.float32(up), jnp.float32(down))


def swap(x):
    even = lax.broadcasted_iota(jnp.int32, x.shape, x.ndim - 2) % 2 == 0
    return jnp.where(even, pltpu.roll(x, 7, x.ndim - 2), pltpu.roll(x, 1, x.ndim - 2))


def split(x):
    high = x.astype(jnp.bfloat16)
    low = (x - high.astype(jnp.float32)).astype(jnp.bfloat16)
    return jnp.concatenate([high, low], axis=0)


def kernel(
    adjoint, jacobian, source, area, band, owner, result,
    own, jac, src, sibling, outbox, inbox, raw, relay, area_v, band_v,
    table, index, weighted, part, gathered, half_sum, other_sum, total, means,
    extent, near_sem, local_sem, sent, sib_recv, raw_recv, link_recv, relay_recv, rs_recv, x_recv, ag_recv,
):
    rows, inst = lax.axis_index("rows"), lax.axis_index("inst")
    z, x_hi, y = rows // 8, (rows // 4) % 2, rows % 4
    core = inst % 2
    sender, agent = core == SENDER, core != SENDER
    sibling_id = (rows, inst + 1 - 2 * core)
    link_id = (rows, (inst + 2) % 4)
    across_id = (z * 8 + (1 - x_hi) * 4 + y, inst)
    me = z * 4 + y
    faces = weighted.shape[1]
    half = faces // 2
    face_groups = faces // (4 * LANES)
    face_start = GROUPS - face_groups
    face_middle = face_start + face_groups // 2
    cuts = (
        ((face_start, face_middle), (face_middle, GROUPS), (0, face_start)),
        ((0, RAW), (RAW, RAW + PART), (RAW + PART, GROUPS)),
    )

    def place(k):
        return (z + k // 4) % 4, (y + k % 4) % 4

    def device(k, inst):
        zd, yd = place(k)
        return (zd * 8 + x_hi * 4 + yd, inst)

    def span(n):
        return pl.ds(RAW + n * PART, PART)

    def each(low, high, act):
        def body(k, carry):
            act(k)
            return carry

        lax.fori_loop(low, high, body, 0)

    def fetch(k, a, b):
        return pltpu.make_async_copy(a, b, local_sem.at[k])

    def drain(like, sem):
        pltpu.make_async_copy(like, like, sem).wait()

    def signal(sem, device_id):
        pl.semaphore_signal(sem, inc=1, device_id=device_id, device_id_type=MESH)

    def remote(a, b, send, recv, device_id):
        return pltpu.make_async_remote_copy(
            a, b, send, recv, device_id=device_id, device_id_type=MESH
        )

    def give(pieces):
        for n, (low, high) in enumerate(pieces):
            here = pl.ds(low, high - low)
            remote(adjoint.at[:, here], sibling.at[:, here], sent, sib_recv.at[n], sibling_id).start()

    def given(pieces, n):
        low, high = pieces[n]
        drain(sibling.at[:, pl.ds(low, high - low)], sib_recv.at[n])

    def beyond(other):
        return (rows, (inst + 2) % 4 + other * (1 - 2 * core))

    def raw_to_link(state, other):
        here = state.at[:, pl.ds(0, RAW)]
        return remote(here, raw, sent, raw_recv, beyond(other))

    def to_link(n, other):
        arrival = link_recv.at[n // (PARTS - 1)]
        return remote(outbox.at[other * PARTS + n], inbox.at[n], sent, arrival, beyond(other))

    def to_relay():
        return remote(raw, relay, sent, relay_recv, sibling_id)

    def scatter(k):
        zd, yd = place(k)
        return remote(part.at[zd * 4 + yd], gathered.at[k], sent, rs_recv, device(k, inst))

    slot = 2 * z + y % 2
    served = inst + (y // 2) * (1 - 2 * core)

    def gather(k):
        return remote(total, means.at[slot], sent, ag_recv, device(k, served))

    def keep():
        return pltpu.make_async_copy(total, means.at[slot], ag_recv)

    across = remote(half_sum, other_sum, sent, x_recv, across_id)

    barrier = pltpu.get_barrier_semaphore()

    @pl.when(sender)
    def _():
        signal(barrier, link_id)

    @pl.when(agent)
    def _():
        signal(barrier, sibling_id)
        for k in FAR_FIRST:
            signal(barrier, device(k, inst))
        signal(barrier, across_id)

    front, tail = pl.ds(0, face_start), pl.ds(face_start, face_groups)
    got_front = fetch(0, adjoint.at[:, front], own.at[:, front])
    got_faces = fetch(1, adjoint.at[:, tail], own.at[:, tail])
    got_area = fetch(2, area, area_v)
    got_band = fetch(3, band, band_v)
    got_jac = fetch(4, jacobian, jac)
    got_src = fetch(5, source, src)

    @pl.when(sender)
    def _():
        got_front.start()
        got_faces.start()
        pl.semaphore_wait(barrier, 2)
        signal(near_sem, sibling_id)
        signal(near_sem, link_id)
        raw_to_link(adjoint, 0).start()
        give(cuts[0])
        got_band.start()
        got_jac.start()
        got_src.start()

    @pl.when(agent)
    def _():
        got_band.start()
        got_faces.start()
        got_area.start()
        got_front.start()
        got_jac.start()
        got_src.start()
        pl.semaphore_wait(near_sem, 1)
        give(cuts[1])

    block_row = lax.broadcasted_iota(jnp.int32, (8, LANES), 0)

    def locate(g):
        bands = band_v[pl.ds(4 * g, 1), :]
        for r in range(1, 4):
            bands = jnp.where(block_row < 2 * r, bands, band_v[pl.ds(4 * g + r, 1), :])
        index[g] = bands

    row = owner[0]
    planes = (jnp.maximum(row - 1, 0), jnp.minimum(row, PLANES - 1))
    on_plane = [
        [jnp.where(planes[h] == p, jnp.float32(1), jnp.float32(0)) for p in range(PLANES)]
        for h in range(2)
    ]

    def turned(x, by):
        return x if by % 8 == 0 else pltpu.roll(x, by % 8, 0)

    def weigh(values, top, low, high):
        def group(g):
            blocks = [values[v, face_start + g] for v in range(4)]
            for r in range(4):
                here = pl.ds(pl.multiple_of((4 * g + r) * LANES, LANES), LANES)
                rows = turned(blocks[0], -2 * r)
                for v in range(1, 4):
                    rows = jnp.where(block_row // 2 == v, turned(blocks[v], 2 * v - 2 * r), rows)
                weighted[top : top + 8, here] = rows * area_v[pl.ds(4 * g + r, 1), :]

        each(low, high, group)

    def weigh_last(low, high):
        def group(g):
            mine, other = own[NV - 1, face_start + g], sibling[NV - 1, face_start + g]
            for r in range(4):
                here = pl.ds(pl.multiple_of((4 * g + r) * LANES, LANES), LANES)
                rows = jnp.where(block_row < 2, turned(mine, -2 * r), turned(other, 2 - 2 * r))
                rows = jnp.where(block_row < 4, rows, jnp.where(block_row == 4, 1.0, 0.0))
                weighted[16:24, here] = rows * area_v[pl.ds(4 * g + r, 1), :]

        each(low, high, group)

    @pl.when(agent)
    def _():
        got_band.wait()
        band_lane = lax.broadcasted_iota(jnp.int32, (LANES, BANDS), 1)
        by_face = jnp.transpose(band_v[...])
        for n in range(faces // LANES):
            here = jnp.where(band_lane == by_face[:, n : n + 1], 1.0, 0.0)
            table[n * LANES : (n + 1) * LANES, :] = here.astype(jnp.bfloat16)
        got_area.wait()
        got_faces.wait()
        weigh(own, 0, 0, face_groups)
        sums = []
        for h in range(2):
            given(cuts[0], h)
            low, high = h * (face_groups // 2), (h + 1) * (face_groups // 2)
            weigh(sibling, 8, low, high)
            weigh_last(low, high)
            cut = slice(h * half, (h + 1) * half)
            both = jnp.dot(split(weighted[:, cut]), table[cut, :], preferred_element_type=jnp.float32)
            sums.append(both[0:24] + both[24:48])
        for p in range(PLANES):
            here = sums[0] * on_plane[0][p] + sums[1] * on_plane[1][p]
            for q in range(4):
                cut = slice(LANES * (q % 2), LANES * (q % 2 + 1))
                part[4 * p + q, 0:8] = here[8 * (q // 2) : 8 * (q // 2) + 8, cut]
                part[4 * p + q, 8:16] = here[16:24, cut]
        pl.semaphore_wait(barrier, OWNERS)
        for k in FAR_FIRST:
            scatter(k).start()

    odd = block_row % 2 == 1

    def weights(by_offset):
        return by_offset[0], jnp.where(odd, by_offset[1], by_offset[-1])

    shifts = (-1, 0, 1)
    inner = weights({d: weight_of(d) for d in shifts})
    facing = weights({d: weight_of(4 + d) for d in shifts})
    skew = 2 if SENDER else -2
    for_facing = weights({d: weight_of(skew + d) for d in shifts})
    for_other = weights({d: weight_of(-skew + d) for d in shifts})
    near = weights({d: pick(core == 0, weight_of(2 + d), weight_of(-2 + d)) for d in shifts})
    away = weights({d: pick(core == 0, weight_of(-2 + d), weight_of(2 + d)) for d in shifts})

    def combine(a, b, wa, wb):
        return wa[0] * a + wb[0] * b + swap(wa[1] * a + wb[1] * b)

    @pl.when(sender)
    def _():
        pl.semaphore_wait(near_sem, 1)
        given(cuts[1], 0)
        raw_to_link(sibling, 1).start()
        got_front.wait()
        got_faces.wait()
        for n in range(PARTS):
            if n < 2:
                given(cuts[1], n + 1)

            def mix_instances(v):
                a, b = own[v, span(n)], sibling[v, span(n)]
                outbox[PARTS + n, v] = combine(b, a, facing, for_other)
                outbox[n, v] = combine(a, b, facing, for_facing)

            each(0, NV, mix_instances)
            to_link(n, 1).start()
            to_link(n, 0).start()
        got_band.wait()

    def base(m):
        here = pl.ds(4 * m, 4)
        state = [own[w, here] for w in range(NV)]
        for v in range(NV):
            flux = 0.0
            for w in range(NV):
                block = jac[w, v, pl.ds(2 * m, 2)].astype(jnp.float32).reshape(4, 8, LANES)
                flux = flux + block * state[w]
            coupled = combine(state[v], sibling[v, here], inner, near)
            result[v, here] = state[v] + coupled - pseudo_step * (flux - src[v, here])

    def bases():
        got_jac.wait()
        got_src.wait()
        each(0, GROUPS // 4, base)
        each(0, face_groups, locate)

    @pl.when(sender)
    def _():
        bases()

    @pl.when(agent)
    def _():
        drain(gathered.at[pl.ds(1, OWNERS - 1)], rs_recv)
        sum_here = part[me]
        for k in range(1, OWNERS):
            sum_here = sum_here + gathered[k]
        half_sum[...] = sum_here
        across.start()
        given(cuts[0], 2)
        got_front.wait()
        bases()
        across.wait_recv()
        total[...] = half_sum[...] + other_sum[...]
        for k in FAR_FIRST:
            gather(k).start()

        @pl.when(y >= 2)
        def _():
            gather(0).start()

        @pl.when(y < 2)
        def _():
            keep().start()

    raw_to_link(adjoint, 0).wait_recv()
    to_relay().start()

    def finish(n):
        result[:, span(n)] += inbox[n]

    drain(inbox.at[pl.ds(0, PARTS - 1)], link_recv.at[0])
    each(0, PARTS - 1, finish)

    to_relay().wait_recv()
    for v in range(NV):
        result[v, 0:RAW] += combine(raw[v], relay[v], facing, away)

    odd_wide = lax.broadcasted_iota(jnp.int32, (8, BANDS), 0) % 2 == 1
    drain(means, ag_recv)
    for h in range(2):
        sums = 0.0
        for p in range(PLANES):
            sums += jnp.concatenate([means[2 * p], means[2 * p + 1]], axis=1) * on_plane[h][p]
        total_area = sums[12:13]
        mean = sums / jnp.where(total_area > 0, total_area, 1.0)
        mean = mean * (pseudo_step * coupling_gain)
        last = jnp.where(agent, mean[8:10], mean[10:12])
        by_row = [
            jnp.where(odd_wide, mean[2 * v + 1 : 2 * v + 2], mean[2 * v : 2 * v + 1]) for v in range(4)
        ] + [jnp.where(odd_wide, last[1:2], last[0:1])]

        def mix(n):
            g = h * (face_groups // 2) + n
            here = face_start + g
            band = index[g]
            lane = band % LANES
            for v in range(NV):
                face_mean = jnp.where(
                    band < LANES,
                    jnp.take_along_axis(by_row[v][:, :LANES], lane, axis=1, mode="promise_in_bounds"),
                    jnp.take_along_axis(by_row[v][:, LANES:], lane, axis=1, mode="promise_in_bounds"),
                )
                result[v, here] += own[v, here] * (pseudo_step * coupling_gain) - face_mean

        each(0, face_groups // 2, mix)

    drain(inbox.at[PARTS - 1], link_recv.at[1])
    finish(PARTS - 1)

    shared = NV * (GROUPS + RAW)
    by_sender = shared + 2 * NV * GROUPS
    by_agent = shared + 2 * (2 * OWNERS - 1)

    @pl.when(sender)
    def _():
        drain(extent.at[pl.ds(0, by_sender)], sent)

    @pl.when(jnp.logical_and(agent, y < 2))
    def _():
        drain(extent.at[pl.ds(0, by_agent)], sent)

    @pl.when(jnp.logical_and(agent, y >= 2))
    def _():
        drain(extent.at[pl.ds(0, by_agent + 2)], sent)


def hbm(x):
    return pltpu.with_memory_space_constraint(x, pltpu.HBM)


def fold(x):
    cells = x.shape[2]
    x = x.reshape(2, NV, cells // (4 * LANES), 4, LANES).transpose(1, 2, 3, 0, 4)
    return x.reshape(NV, cells // (4 * LANES), 8, LANES)


def unfold(x):
    x = x.reshape(NV, x.shape[1], 4, 2, LANES).transpose(3, 0, 1, 2, 4)
    return x.reshape(2, NV, -1)


def fold_jacobian(x):
    cells = x.shape[3]
    x = x.reshape(2, NV, NV, cells // (8 * LANES), 8, LANES).transpose(1, 2, 3, 4, 0, 5)
    return x.reshape(NV, NV, cells // (8 * LANES), 16, LANES)


def shards(adjoint, jacobian, source_term, face_area, face_band, partition_row):
    cells, faces = adjoint.shape[2], face_area.shape[0]
    groups = cells // (4 * LANES)
    assert groups == GROUPS
    f32, bf16, i32 = jnp.float32, jnp.bfloat16, jnp.int32
    dma = pltpu.SemaphoreType.DMA
    state = pltpu.VMEM((NV, groups, 8, LANES), f32)
    box = pltpu.VMEM((16, LANES), f32)
    boxes = pltpu.VMEM((OWNERS, 16, LANES), f32)
    updated = pl.pallas_call(
        kernel,
        out_shape=pltpu.VMEM((NV, groups, 8, LANES), f32),
        in_specs=[pl.BlockSpec(memory_space=pl.ANY)] * 5 + [pl.BlockSpec(memory_space=pltpu.SMEM)],
        out_specs=pl.BlockSpec(memory_space=pltpu.VMEM),
        scratch_shapes=[
            state,
            pltpu.VMEM((NV, NV, groups // 2, 16, LANES), bf16),
            state,
            state,
            pltpu.VMEM((2 * PARTS, NV, PART, 8, LANES), f32),
            pltpu.VMEM((PARTS, NV, PART, 8, LANES), f32),
            pltpu.VMEM((NV, RAW, 8, LANES), f32),
            pltpu.VMEM((NV, RAW, 8, LANES), f32),
            pltpu.VMEM((faces // LANES, LANES), f32),
            pltpu.VMEM((faces // LANES, LANES), i32),
            pltpu.VMEM((faces, BANDS), bf16),
            pltpu.VMEM((faces // (4 * LANES), 8, LANES), i32),
            pltpu.VMEM((24, faces), f32),
            boxes,
            boxes,
            box,
            box,
            box,
            pltpu.VMEM((OWNERS // 2, 16, LANES), f32),
            pltpu.VMEM((NV * (3 * GROUPS + RAW), 8, LANES), f32),
            pltpu.SemaphoreType.REGULAR,
            dma((6,)),
            dma,
            dma((3,)),
            dma,
            dma((2,)),
            dma,
            dma,
            dma,
            dma,
        ],
        compiler_params=pltpu.CompilerParams(
            collective_id=0, has_side_effects=True, vmem_limit_bytes=40 << 20
        ),
    )(
        hbm(fold(adjoint)),
        hbm(fold_jacobian(jacobian)),
        hbm(fold(source_term)),
        hbm(face_area.reshape(faces // LANES, LANES)),
        hbm(face_band.reshape(faces // LANES, LANES)),
        partition_row,
    )
    return unfold(updated)


def solution(mesh):
    placed = (
        P("inst", None, "rows"),
        P("inst", None, None, "rows"),
        P("inst", None, "rows"),
        P("rows"),
        P("rows"),
        P("rows"),
    )
    return jax.shard_map(
        shards, mesh=mesh, in_specs=placed, out_specs=P("inst", None, "rows"), check_vma=False
    )
```

```python
import jax
import jax.numpy as jnp
import numpy as np
from jax import lax
from jax.experimental import pallas as pl
from jax.experimental.pallas import tpu as pltpu
from jax.sharding import PartitionSpec as P

MESH = pl.DeviceIdType.MESH
NT = 8
NV = 5
NB = 200
PLANES = 4
BANDS = 256
LANES = 128

frequency = 1.0
coupling_gain = 2.0
pseudo_step = 0.5

SENDER = 0
GROUPS = 36
RAW = 8
PARTS = 4
PART = (GROUPS - RAW) // PARTS
OWNERS = 16


def ring(k):
    return min(k, 4 - k)


FAR_FIRST = sorted(range(1, OWNERS), key=lambda k: -ring(k // 4) - ring(k % 4))


def spectral(offset):
    if offset % NT == 0:
        return 0.0
    angle = np.float32(np.pi * offset / NT)
    return float(np.float32(0.5 * (-1) ** (offset % 2)) / np.tan(angle))


def weight_of(offset):
    return -pseudo_step * frequency * spectral(offset)


def pick(first, up, down):
    return jnp.where(first, jnp.float32(up), jnp.float32(down))


def swap(x):
    even = lax.broadcasted_iota(jnp.int32, x.shape, x.ndim - 2) % 2 == 0
    return jnp.where(even, pltpu.roll(x, 7, x.ndim - 2), pltpu.roll(x, 1, x.ndim - 2))


def split(x):
    high = x.astype(jnp.bfloat16)
    low = (x - high.astype(jnp.float32)).astype(jnp.bfloat16)
    return jnp.concatenate([high, low], axis=0)


def kernel(
    adjoint, jacobian, source, area, band, owner, result,
    own, jac, src, sibling, outbox, inbox, raw, relay, area_v, band_v,
    table, index, weighted, part, gathered, half_sum, other_sum, total, means,
    extent, near_sem, local_sem, sent, sib_recv, raw_recv, link_recv, relay_recv, rs_recv, x_recv, ag_recv,
):
    rows, inst = lax.axis_index("rows"), lax.axis_index("inst")
    z, x_hi, y = rows // 8, (rows // 4) % 2, rows % 4
    core = inst % 2
    sender, agent = core == SENDER, core != SENDER
    sibling_id = (rows, inst + 1 - 2 * core)
    link_id = (rows, (inst + 2) % 4)
    across_id = (z * 8 + (1 - x_hi) * 4 + y, inst)
    me = z * 4 + y
    faces = weighted.shape[1]
    half = faces // 2
    face_groups = faces // (4 * LANES)
    face_start = GROUPS - face_groups
    face_middle = face_start + face_groups // 2
    cuts = (
        ((face_start, face_middle), (face_middle, GROUPS), (0, face_start)),
        ((0, RAW), (RAW, RAW + PART), (RAW + PART, GROUPS)),
    )

    def place(k):
        return (z + k // 4) % 4, (y + k % 4) % 4

    def device(k, inst):
        zd, yd = place(k)
        return (zd * 8 + x_hi * 4 + yd, inst)

    def span(n):
        return pl.ds(RAW + n * PART, PART)

    def each(low, high, act):
        def body(k, carry):
            act(k)
            return carry

        lax.fori_loop(low, high, body, 0)

    def fetch(k, a, b):
        return pltpu.make_async_copy(a, b, local_sem.at[k])

    def drain(like, sem):
        pltpu.make_async_copy(like, like, sem).wait()

    def signal(sem, device_id):
        pl.semaphore_signal(sem, inc=1, device_id=device_id, device_id_type=MESH)

    def remote(a, b, send, recv, device_id):
        return pltpu.make_async_remote_copy(
            a, b, send, recv, device_id=device_id, device_id_type=MESH
        )

    def give(pieces):
        for n, (low, high) in enumerate(pieces):
            here = pl.ds(low, high - low)
            remote(adjoint.at[:, here], sibling.at[:, here], sent, sib_recv.at[n], sibling_id).start()

    def given(pieces, n):
        low, high = pieces[n]
        drain(sibling.at[:, pl.ds(low, high - low)], sib_recv.at[n])

    def beyond(other):
        return (rows, (inst + 2) % 4 + other * (1 - 2 * core))

    def raw_to_link(state, other):
        here = state.at[:, pl.ds(0, RAW)]
        return remote(here, raw, sent, raw_recv, beyond(other))

    def to_link(n, other):
        arrival = link_recv.at[n // (PARTS - 1)]
        return remote(outbox.at[other * PARTS + n], inbox.at[n], sent, arrival, beyond(other))

    def to_relay():
        return remote(raw, relay, sent, relay_recv, sibling_id)

    def scatter(k):
        zd, yd = place(k)
        return remote(part.at[zd * 4 + yd], gathered.at[k], sent, rs_recv, device(k, inst))

    slot = 2 * z + y % 2
    served = inst + (y // 2) * (1 - 2 * core)

    def gather(k):
        return remote(total, means.at[slot], sent, ag_recv, device(k, served))

    def keep():
        return pltpu.make_async_copy(total, means.at[slot], ag_recv)

    across = remote(half_sum, other_sum, sent, x_recv, across_id)

    barrier = pltpu.get_barrier_semaphore()

    @pl.when(sender)
    def _():
        signal(barrier, link_id)

    @pl.when(agent)
    def _():
        signal(barrier, sibling_id)
        for k in FAR_FIRST:
            signal(barrier, device(k, inst))
        signal(barrier, across_id)

    front, tail = pl.ds(0, face_start), pl.ds(face_start, face_groups)
    got_front = fetch(0, adjoint.at[:, front], own.at[:, front])
    got_faces = fetch(1, adjoint.at[:, tail], own.at[:, tail])
    got_area = fetch(2, area, area_v)
    got_band = fetch(3, band, band_v)
    got_jac = fetch(4, jacobian, jac)
    got_src = fetch(5, source, src)

    @pl.when(sender)
    def _():
        got_front.start()
        got_faces.start()
        pl.semaphore_wait(barrier, 2)
        raw_to_link(adjoint, 0).start()
        signal(near_sem, sibling_id)
        signal(near_sem, link_id)
        give(cuts[0])
        got_band.start()
        got_jac.start()
        got_src.start()

    @pl.when(agent)
    def _():
        got_band.start()
        got_faces.start()
        got_area.start()
        got_front.start()
        got_jac.start()
        got_src.start()
        pl.semaphore_wait(near_sem, 1)
        give(cuts[1])

    block_row = lax.broadcasted_iota(jnp.int32, (8, LANES), 0)

    def locate(g):
        bands = band_v[pl.ds(4 * g, 1), :]
        for r in range(1, 4):
            bands = jnp.where(block_row < 2 * r, bands, band_v[pl.ds(4 * g + r, 1), :])
        index[g] = bands

    row = owner[0]
    planes = (jnp.maximum(row - 1, 0), jnp.minimum(row, PLANES - 1))
    on_plane = [
        [jnp.where(planes[h] == p, jnp.float32(1), jnp.float32(0)) for p in range(PLANES)]
        for h in range(2)
    ]

    def turned(x, by):
        return x if by % 8 == 0 else pltpu.roll(x, by % 8, 0)

    def weigh(values, top, low, high):
        def group(g):
            blocks = [values[v, face_start + g] for v in range(4)]
            for r in range(4):
                here = pl.ds(pl.multiple_of((4 * g + r) * LANES, LANES), LANES)
                rows = turned(blocks[0], -2 * r)
                for v in range(1, 4):
                    rows = jnp.where(block_row // 2 == v, turned(blocks[v], 2 * v - 2 * r), rows)
                weighted[top : top + 8, here] = rows * area_v[pl.ds(4 * g + r, 1), :]

        each(low, high, group)

    def weigh_last(low, high):
        def group(g):
            mine, other = own[NV - 1, face_start + g], sibling[NV - 1, face_start + g]
            for r in range(4):
                here = pl.ds(pl.multiple_of((4 * g + r) * LANES, LANES), LANES)
                rows = jnp.where(block_row < 2, turned(mine, -2 * r), turned(other, 2 - 2 * r))
                rows = jnp.where(block_row < 4, rows, jnp.where(block_row == 4, 1.0, 0.0))
                weighted[16:24, here] = rows * area_v[pl.ds(4 * g + r, 1), :]

        each(low, high, group)

    @pl.when(agent)
    def _():
        got_band.wait()
        band_lane = lax.broadcasted_iota(jnp.int32, (LANES, BANDS), 1)
        by_face = jnp.transpose(band_v[...])

        def mark(h):
            tiles = half // LANES
            for n in range(h * tiles, (h + 1) * tiles):
                here = jnp.where(band_lane == by_face[:, n : n + 1], 1.0, 0.0)
                table[n * LANES : (n + 1) * LANES, :] = here.astype(jnp.bfloat16)

        mark(0)
        got_area.wait()
        got_faces.wait()
        weigh(own, 0, 0, face_groups)
        sums = []
        for h in range(2):
            given(cuts[0], h)
            low, high = h * (face_groups // 2), (h + 1) * (face_groups // 2)
            weigh(sibling, 8, low, high)
            weigh_last(low, high)
            cut = slice(h * half, (h + 1) * half)
            both = jnp.dot(split(weighted[:, cut]), table[cut, :], preferred_element_type=jnp.float32)
            sums.append(both[0:24] + both[24:48])
            if h == 0:
                mark(1)
        for p in range(PLANES):
            here = sums[0] * on_plane[0][p] + sums[1] * on_plane[1][p]
            for q in range(4):
                cut = slice(LANES * (q % 2), LANES * (q % 2 + 1))
                part[4 * p + q, 0:8] = here[8 * (q // 2) : 8 * (q // 2) + 8, cut]
                part[4 * p + q, 8:16] = here[16:24, cut]
        pl.semaphore_wait(barrier, OWNERS)
        for k in FAR_FIRST:
            scatter(k).start()

    odd = block_row % 2 == 1

    def weights(by_offset):
        return by_offset[0], jnp.where(odd, by_offset[1], by_offset[-1])

    shifts = (-1, 0, 1)
    inner = weights({d: weight_of(d) for d in shifts})
    facing = weights({d: weight_of(4 + d) for d in shifts})
    skew = 2 if SENDER else -2
    for_facing = weights({d: weight_of(skew + d) for d in shifts})
    for_other = weights({d: weight_of(-skew + d) for d in shifts})
    near = weights({d: pick(core == 0, weight_of(2 + d), weight_of(-2 + d)) for d in shifts})
    away = weights({d: pick(core == 0, weight_of(-2 + d), weight_of(2 + d)) for d in shifts})

    def combine(a, b, wa, wb):
        return wa[0] * a + wb[0] * b + swap(wa[1] * a + wb[1] * b)

    @pl.when(sender)
    def _():
        pl.semaphore_wait(near_sem, 1)
        given(cuts[1], 0)
        raw_to_link(sibling, 1).start()
        got_front.wait()
        got_faces.wait()
        for n in range(PARTS):
            if n < 2:
                given(cuts[1], n + 1)

            def mix_instances(v):
                a, b = own[v, span(n)], sibling[v, span(n)]
                outbox[PARTS + n, v] = combine(b, a, facing, for_other)
                outbox[n, v] = combine(a, b, facing, for_facing)

            each(0, NV, mix_instances)
            to_link(n, 1).start()
            to_link(n, 0).start()
        got_band.wait()

    def base(m):
        here = pl.ds(4 * m, 4)
        state = [own[w, here] for w in range(NV)]
        for v in range(NV):
            flux = 0.0
            for w in range(NV):
                block = jac[w, v, pl.ds(2 * m, 2)].astype(jnp.float32).reshape(4, 8, LANES)
                flux = flux + block * state[w]
            coupled = combine(state[v], sibling[v, here], inner, near)
            result[v, here] = state[v] + coupled - pseudo_step * (flux - src[v, here])

    def bases():
        got_jac.wait()
        got_src.wait()
        each(0, GROUPS // 4, base)
        each(0, face_groups, locate)

    @pl.when(sender)
    def _():
        bases()

    @pl.when(agent)
    def _():
        drain(gathered.at[pl.ds(1, OWNERS - 1)], rs_recv)
        sum_here = part[me]
        for k in range(1, OWNERS):
            sum_here = sum_here + gathered[k]
        half_sum[...] = sum_here
        across.start()
        given(cuts[0], 2)
        got_front.wait()
        bases()
        across.wait_recv()
        total[...] = half_sum[...] + other_sum[...]
        for k in FAR_FIRST:
            gather(k).start()

        @pl.when(y >= 2)
        def _():
            gather(0).start()

        @pl.when(y < 2)
        def _():
            keep().start()

    raw_to_link(adjoint, 0).wait_recv()
    to_relay().start()

    def finish(n):
        result[:, span(n)] += inbox[n]

    drain(inbox.at[pl.ds(0, PARTS - 1)], link_recv.at[0])
    each(0, PARTS - 1, finish)

    to_relay().wait_recv()
    for v in range(NV):
        result[v, 0:RAW] += combine(raw[v], relay[v], facing, away)

    odd_wide = lax.broadcasted_iota(jnp.int32, (8, BANDS), 0) % 2 == 1
    drain(means, ag_recv)
    for h in range(2):
        sums = 0.0
        for p in range(PLANES):
            sums += jnp.concatenate([means[2 * p], means[2 * p + 1]], axis=1) * on_plane[h][p]
        total_area = sums[12:13]
        mean = sums / jnp.where(total_area > 0, total_area, 1.0)
        mean = mean * (pseudo_step * coupling_gain)
        last = jnp.where(agent, mean[8:10], mean[10:12])
        by_row = [
            jnp.where(odd_wide, mean[2 * v + 1 : 2 * v + 2], mean[2 * v : 2 * v + 1]) for v in range(4)
        ] + [jnp.where(odd_wide, last[1:2], last[0:1])]

        def mix(n):
            g = h * (face_groups // 2) + n
            here = face_start + g
            band = index[g]
            lane = band % LANES
            for v in range(NV):
                face_mean = jnp.where(
                    band < LANES,
                    jnp.take_along_axis(by_row[v][:, :LANES], lane, axis=1, mode="promise_in_bounds"),
                    jnp.take_along_axis(by_row[v][:, LANES:], lane, axis=1, mode="promise_in_bounds"),
                )
                result[v, here] += own[v, here] * (pseudo_step * coupling_gain) - face_mean

        each(0, face_groups // 2, mix)

    drain(inbox.at[PARTS - 1], link_recv.at[1])
    finish(PARTS - 1)

    shared = NV * (GROUPS + RAW)
    by_sender = shared + 2 * NV * GROUPS
    by_agent = shared + 2 * (2 * OWNERS - 1)

    @pl.when(sender)
    def _():
        drain(extent.at[pl.ds(0, by_sender)], sent)

    @pl.when(jnp.logical_and(agent, y < 2))
    def _():
        drain(extent.at[pl.ds(0, by_agent)], sent)

    @pl.when(jnp.logical_and(agent, y >= 2))
    def _():
        drain(extent.at[pl.ds(0, by_agent + 2)], sent)


def hbm(x):
    return pltpu.with_memory_space_constraint(x, pltpu.HBM)


def fold(x):
    cells = x.shape[2]
    x = x.reshape(2, NV, cells // (4 * LANES), 4, LANES).transpose(1, 2, 3, 0, 4)
    return x.reshape(NV, cells // (4 * LANES), 8, LANES)


def unfold(x):
    x = x.reshape(NV, x.shape[1], 4, 2, LANES).transpose(3, 0, 1, 2, 4)
    return x.reshape(2, NV, -1)


def fold_jacobian(x):
    cells = x.shape[3]
    x = x.reshape(2, NV, NV, cells // (8 * LANES), 8, LANES).transpose(1, 2, 3, 4, 0, 5)
    return x.reshape(NV, NV, cells // (8 * LANES), 16, LANES)


def shards(adjoint, jacobian, source_term, face_area, face_band, partition_row):
    cells, faces = adjoint.shape[2], face_area.shape[0]
    groups = cells // (4 * LANES)
    assert groups == GROUPS
    f32, bf16, i32 = jnp.float32, jnp.bfloat16, jnp.int32
    dma = pltpu.SemaphoreType.DMA
    state = pltpu.VMEM((NV, groups, 8, LANES), f32)
    box = pltpu.VMEM((16, LANES), f32)
    boxes = pltpu.VMEM((OWNERS, 16, LANES), f32)
    updated = pl.pallas_call(
        kernel,
        out_shape=pltpu.VMEM((NV, groups, 8, LANES), f32),
        in_specs=[pl.BlockSpec(memory_space=pl.ANY)] * 5 + [pl.BlockSpec(memory_space=pltpu.SMEM)],
        out_specs=pl.BlockSpec(memory_space=pltpu.VMEM),
        scratch_shapes=[
            state,
            pltpu.VMEM((NV, NV, groups // 2, 16, LANES), bf16),
            state,
            state,
            pltpu.VMEM((2 * PARTS, NV, PART, 8, LANES), f32),
            pltpu.VMEM((PARTS, NV, PART, 8, LANES), f32),
            pltpu.VMEM((NV, RAW, 8, LANES), f32),
            pltpu.VMEM((NV, RAW, 8, LANES), f32),
            pltpu.VMEM((faces // LANES, LANES), f32),
            pltpu.VMEM((faces // LANES, LANES), i32),
            pltpu.VMEM((faces, BANDS), bf16),
            pltpu.VMEM((faces // (4 * LANES), 8, LANES), i32),
            pltpu.VMEM((24, faces), f32),
            boxes,
            boxes,
            box,
            box,
            box,
            pltpu.VMEM((OWNERS // 2, 16, LANES), f32),
            pltpu.VMEM((NV * (3 * GROUPS + RAW), 8, LANES), f32),
            pltpu.SemaphoreType.REGULAR,
            dma((6,)),
            dma,
            dma((3,)),
            dma,
            dma((2,)),
            dma,
            dma,
            dma,
            dma,
        ],
        compiler_params=pltpu.CompilerParams(
            collective_id=0, has_side_effects=True, vmem_limit_bytes=40 << 20
        ),
    )(
        hbm(fold(adjoint)),
        hbm(fold_jacobian(jacobian)),
        hbm(fold(source_term)),
        hbm(face_area.reshape(faces // LANES, LANES)),
        hbm(face_band.reshape(faces // LANES, LANES)),
        partition_row,
    )
    return unfold(updated)


def solution(mesh):
    placed = (
        P("inst", None, "rows"),
        P("inst", None, None, "rows"),
        P("inst", None, "rows"),
        P("rows"),
        P("rows"),
        P("rows"),
    )
    return jax.shard_map(
        shards, mesh=mesh, in_specs=placed, out_specs=P("inst", None, "rows"), check_vma=False
    )
```

```python
import jax
import jax.numpy as jnp
import numpy as np
from jax import lax
from jax.experimental import pallas as pl
from jax.experimental.pallas import tpu as pltpu
from jax.sharding import PartitionSpec as P

MESH = pl.DeviceIdType.MESH
NT = 8
NV = 5
NB = 200
PLANES = 4
BANDS = 256
LANES = 128

frequency = 1.0
coupling_gain = 2.0
pseudo_step = 0.5

SENDER = 0
GROUPS = 36
RAW = 8
PARTS = 4
PART = (GROUPS - RAW) // PARTS
OWNERS = 16


def ring(k):
    return min(k, 4 - k)


FAR_FIRST = sorted(range(1, OWNERS), key=lambda k: -ring(k // 4) - ring(k % 4))


def spectral(offset):
    if offset % NT == 0:
        return 0.0
    angle = np.float32(np.pi * offset / NT)
    return float(np.float32(0.5 * (-1) ** (offset % 2)) / np.tan(angle))


def weight_of(offset):
    return -pseudo_step * frequency * spectral(offset)


def pick(first, up, down):
    return jnp.where(first, jnp.float32(up), jnp.float32(down))


def swap(x):
    even = lax.broadcasted_iota(jnp.int32, x.shape, x.ndim - 2) % 2 == 0
    return jnp.where(even, pltpu.roll(x, 7, x.ndim - 2), pltpu.roll(x, 1, x.ndim - 2))


def split(x):
    high = x.astype(jnp.bfloat16)
    low = (x - high.astype(jnp.float32)).astype(jnp.bfloat16)
    return jnp.concatenate([high, low], axis=0)


def kernel(
    adjoint, jacobian, source, area, band, owner, result,
    own, jac, src, sibling, outbox, inbox, raw, relay, area_v, band_v,
    table, index, weighted, part, gathered, half_sum, other_sum, total, means,
    extent, near_sem, local_sem, sent, sib_recv, raw_recv, link_recv, relay_recv, rs_recv, x_recv, ag_recv,
):
    rows, inst = lax.axis_index("rows"), lax.axis_index("inst")
    z, x_hi, y = rows // 8, (rows // 4) % 2, rows % 4
    core = inst % 2
    sender, agent = core == SENDER, core != SENDER
    sibling_id = (rows, inst + 1 - 2 * core)
    link_id = (rows, (inst + 2) % 4)
    across_id = (z * 8 + (1 - x_hi) * 4 + y, inst)
    me = z * 4 + y
    faces = weighted.shape[1]
    half = faces // 2
    face_groups = faces // (4 * LANES)
    face_start = GROUPS - face_groups
    face_middle = face_start + face_groups // 2
    cuts = (
        ((face_start, face_middle), (face_middle, GROUPS), (0, face_start)),
        ((0, RAW), (RAW, RAW + PART), (RAW + PART, GROUPS)),
    )

    def place(k):
        return (z + k // 4) % 4, (y + k % 4) % 4

    def device(k, inst):
        zd, yd = place(k)
        return (zd * 8 + x_hi * 4 + yd, inst)

    def span(n):
        return pl.ds(RAW + n * PART, PART)

    def each(low, high, act):
        def body(k, carry):
            act(k)
            return carry

        lax.fori_loop(low, high, body, 0)

    def fetch(k, a, b):
        return pltpu.make_async_copy(a, b, local_sem.at[k])

    def drain(like, sem):
        pltpu.make_async_copy(like, like, sem).wait()

    def signal(sem, device_id):
        pl.semaphore_signal(sem, inc=1, device_id=device_id, device_id_type=MESH)

    def remote(a, b, send, recv, device_id):
        return pltpu.make_async_remote_copy(
            a, b, send, recv, device_id=device_id, device_id_type=MESH
        )

    def give(pieces):
        for n, (low, high) in enumerate(pieces):
            here = pl.ds(low, high - low)
            remote(adjoint.at[:, here], sibling.at[:, here], sent, sib_recv.at[n], sibling_id).start()

    def given(pieces, n):
        low, high = pieces[n]
        drain(sibling.at[:, pl.ds(low, high - low)], sib_recv.at[n])

    def beyond(other):
        return (rows, (inst + 2) % 4 + other * (1 - 2 * core))

    def raw_to_link(state, other):
        here = state.at[:, pl.ds(0, RAW)]
        return remote(here, raw, sent, raw_recv, beyond(other))

    def to_link(n, other):
        arrival = link_recv.at[n // (PARTS - 1)]
        return remote(outbox.at[other * PARTS + n], inbox.at[n], sent, arrival, beyond(other))

    def to_relay():
        return remote(raw, relay, sent, relay_recv, sibling_id)

    def scatter(k):
        zd, yd = place(k)
        return remote(part.at[zd * 4 + yd], gathered.at[k], sent, rs_recv, device(k, inst))

    slot = 2 * z + y % 2
    served = inst + (y // 2) * (1 - 2 * core)

    def gather(k):
        return remote(total, means.at[slot], sent, ag_recv, device(k, served))

    def keep():
        return pltpu.make_async_copy(total, means.at[slot], ag_recv)

    across = remote(half_sum, other_sum, sent, x_recv, across_id)

    barrier = pltpu.get_barrier_semaphore()

    @pl.when(sender)
    def _():
        signal(barrier, link_id)

    @pl.when(agent)
    def _():
        signal(barrier, sibling_id)
        for k in FAR_FIRST:
            signal(barrier, device(k, inst))
        signal(barrier, across_id)

    front, tail = pl.ds(0, face_start), pl.ds(face_start, face_groups)
    got_front = fetch(0, adjoint.at[:, front], own.at[:, front])
    got_faces = fetch(1, adjoint.at[:, tail], own.at[:, tail])
    got_area = fetch(2, area, area_v)
    got_band = fetch(3, band, band_v)
    got_jac = fetch(4, jacobian, jac)
    got_src = fetch(5, source, src)

    @pl.when(sender)
    def _():
        got_front.start()
        got_faces.start()
        pl.semaphore_wait(barrier, 2)
        signal(near_sem, sibling_id)
        signal(near_sem, link_id)
        raw_to_link(adjoint, 0).start()
        give(cuts[0])
        got_band.start()
        got_jac.start()
        got_src.start()

    @pl.when(agent)
    def _():
        got_band.start()
        got_faces.start()
        got_area.start()
        got_front.start()
        got_jac.start()
        got_src.start()
        pl.semaphore_wait(near_sem, 1)
        give(cuts[1])

    block_row = lax.broadcasted_iota(jnp.int32, (8, LANES), 0)

    def locate(g):
        bands = band_v[pl.ds(4 * g, 1), :]
        for r in range(1, 4):
            bands = jnp.where(block_row < 2 * r, bands, band_v[pl.ds(4 * g + r, 1), :])
        index[g] = bands
        here = face_start + g
        for v in range(NV):
            result[v, here] += own[v, here] * (pseudo_step * coupling_gain)

    row = owner[0]
    planes = (jnp.maximum(row - 1, 0), jnp.minimum(row, PLANES - 1))
    on_plane = [
        [jnp.where(planes[h] == p, jnp.float32(1), jnp.float32(0)) for p in range(PLANES)]
        for h in range(2)
    ]

    def turned(x, by):
        return x if by % 8 == 0 else pltpu.roll(x, by % 8, 0)

    def weigh(values, top, low, high):
        def group(g):
            blocks = [values[v, face_start + g] for v in range(4)]
            for r in range(4):
                here = pl.ds(pl.multiple_of((4 * g + r) * LANES, LANES), LANES)
                rows = turned(blocks[0], -2 * r)
                for v in range(1, 4):
                    rows = jnp.where(block_row // 2 == v, turned(blocks[v], 2 * v - 2 * r), rows)
                weighted[top : top + 8, here] = rows * area_v[pl.ds(4 * g + r, 1), :]

        each(low, high, group)

    def weigh_last(low, high):
        def group(g):
            mine, other = own[NV - 1, face_start + g], sibling[NV - 1, face_start + g]
            for r in range(4):
                here = pl.ds(pl.multiple_of((4 * g + r) * LANES, LANES), LANES)
                rows = jnp.where(block_row < 2, turned(mine, -2 * r), turned(other, 2 - 2 * r))
                rows = jnp.where(block_row < 4, rows, jnp.where(block_row == 4, 1.0, 0.0))
                weighted[16:24, here] = rows * area_v[pl.ds(4 * g + r, 1), :]

        each(low, high, group)

    @pl.when(agent)
    def _():
        got_band.wait()
        band_lane = lax.broadcasted_iota(jnp.int32, (LANES, BANDS), 1)
        by_face = jnp.transpose(band_v[...])
        for n in range(faces // LANES):
            here = jnp.where(band_lane == by_face[:, n : n + 1], 1.0, 0.0)
            table[n * LANES : (n + 1) * LANES, :] = here.astype(jnp.bfloat16)
        got_area.wait()
        got_faces.wait()
        weigh(own, 0, 0, face_groups)
        sums = []
        for h in range(2):
            given(cuts[0], h)
            low, high = h * (face_groups // 2), (h + 1) * (face_groups // 2)
            weigh(sibling, 8, low, high)
            weigh_last(low, high)
            cut = slice(h * half, (h + 1) * half)
            both = jnp.dot(split(weighted[:, cut]), table[cut, :], preferred_element_type=jnp.float32)
            sums.append(both[0:24] + both[24:48])
        for p in range(PLANES):
            here = sums[0] * on_plane[0][p] + sums[1] * on_plane[1][p]
            for q in range(4):
                cut = slice(LANES * (q % 2), LANES * (q % 2 + 1))
                part[4 * p + q, 0:8] = here[8 * (q // 2) : 8 * (q // 2) + 8, cut]
                part[4 * p + q, 8:16] = here[16:24, cut]
        pl.semaphore_wait(barrier, OWNERS)
        for k in FAR_FIRST:
            scatter(k).start()

    odd = block_row % 2 == 1

    def weights(by_offset):
        return by_offset[0], jnp.where(odd, by_offset[1], by_offset[-1])

    shifts = (-1, 0, 1)
    inner = weights({d: weight_of(d) for d in shifts})
    facing = weights({d: weight_of(4 + d) for d in shifts})
    skew = 2 if SENDER else -2
    for_facing = weights({d: weight_of(skew + d) for d in shifts})
    for_other = weights({d: weight_of(-skew + d) for d in shifts})
    near = weights({d: pick(core == 0, weight_of(2 + d), weight_of(-2 + d)) for d in shifts})
    away = weights({d: pick(core == 0, weight_of(-2 + d), weight_of(2 + d)) for d in shifts})

    def combine(a, b, wa, wb):
        return wa[0] * a + wb[0] * b + swap(wa[1] * a + wb[1] * b)

    @pl.when(sender)
    def _():
        pl.semaphore_wait(near_sem, 1)
        given(cuts[1], 0)
        raw_to_link(sibling, 1).start()
        got_front.wait()
        got_faces.wait()
        for n in range(PARTS):
            if n < 2:
                given(cuts[1], n + 1)

            def mix_instances(v):
                a, b = own[v, span(n)], sibling[v, span(n)]
                outbox[PARTS + n, v] = combine(b, a, facing, for_other)
                outbox[n, v] = combine(a, b, facing, for_facing)

            each(0, NV, mix_instances)
            to_link(n, 1).start()
            to_link(n, 0).start()
        got_band.wait()

    def base(m):
        here = pl.ds(4 * m, 4)
        state = [own[w, here] for w in range(NV)]
        for v in range(NV):
            flux = 0.0
            for w in range(NV):
                block = jac[w, v, pl.ds(2 * m, 2)].astype(jnp.float32).reshape(4, 8, LANES)
                flux = flux + block * state[w]
            coupled = combine(state[v], sibling[v, here], inner, near)
            result[v, here] = state[v] + coupled - pseudo_step * (flux - src[v, here])

    def bases():
        got_jac.wait()
        got_src.wait()
        each(0, GROUPS // 4, base)
        each(0, face_groups, locate)

    @pl.when(sender)
    def _():
        bases()

    @pl.when(agent)
    def _():
        drain(gathered.at[pl.ds(1, OWNERS - 1)], rs_recv)
        sum_here = part[me]
        for k in range(1, OWNERS):
            sum_here = sum_here + gathered[k]
        half_sum[...] = sum_here
        across.start()
        given(cuts[0], 2)
        got_front.wait()
        bases()
        across.wait_recv()
        total[...] = half_sum[...] + other_sum[...]
        for k in FAR_FIRST:
            gather(k).start()

        @pl.when(y >= 2)
        def _():
            gather(0).start()

        @pl.when(y < 2)
        def _():
            keep().start()

    raw_to_link(adjoint, 0).wait_recv()
    to_relay().start()

    def finish(n):
        result[:, span(n)] += inbox[n]

    drain(inbox.at[pl.ds(0, PARTS - 1)], link_recv.at[0])
    each(0, PARTS - 1, finish)

    to_relay().wait_recv()
    for v in range(NV):
        result[v, 0:RAW] += combine(raw[v], relay[v], facing, away)

    odd_wide = lax.broadcasted_iota(jnp.int32, (8, BANDS), 0) % 2 == 1
    drain(means, ag_recv)
    for h in range(2):
        sums = 0.0
        for p in range(PLANES):
            sums += jnp.concatenate([means[2 * p], means[2 * p + 1]], axis=1) * on_plane[h][p]
        total_area = sums[12:13]
        mean = sums / jnp.where(total_area > 0, total_area, 1.0)
        mean = mean * (pseudo_step * coupling_gain)
        last = jnp.where(agent, mean[8:10], mean[10:12])
        by_row = [
            jnp.where(odd_wide, mean[2 * v + 1 : 2 * v + 2], mean[2 * v : 2 * v + 1]) for v in range(4)
        ] + [jnp.where(odd_wide, last[1:2], last[0:1])]

        def mix(n):
            g = h * (face_groups // 2) + n
            here = face_start + g
            band = index[g]
            lane = band % LANES
            for v in range(NV):
                face_mean = jnp.where(
                    band < LANES,
                    jnp.take_along_axis(by_row[v][:, :LANES], lane, axis=1, mode="promise_in_bounds"),
                    jnp.take_along_axis(by_row[v][:, LANES:], lane, axis=1, mode="promise_in_bounds"),
                )
                result[v, here] -= face_mean

        each(0, face_groups // 2, mix)

    drain(inbox.at[PARTS - 1], link_recv.at[1])
    finish(PARTS - 1)

    shared = NV * (GROUPS + RAW)
    by_sender = shared + 2 * NV * GROUPS
    by_agent = shared + 2 * (2 * OWNERS - 1)

    @pl.when(sender)
    def _():
        drain(extent.at[pl.ds(0, by_sender)], sent)

    @pl.when(jnp.logical_and(agent, y < 2))
    def _():
        drain(extent.at[pl.ds(0, by_agent)], sent)

    @pl.when(jnp.logical_and(agent, y >= 2))
    def _():
        drain(extent.at[pl.ds(0, by_agent + 2)], sent)


def hbm(x):
    return pltpu.with_memory_space_constraint(x, pltpu.HBM)


def fold(x):
    cells = x.shape[2]
    x = x.reshape(2, NV, cells // (4 * LANES), 4, LANES).transpose(1, 2, 3, 0, 4)
    return x.reshape(NV, cells // (4 * LANES), 8, LANES)


def unfold(x):
    x = x.reshape(NV, x.shape[1], 4, 2, LANES).transpose(3, 0, 1, 2, 4)
    return x.reshape(2, NV, -1)


def fold_jacobian(x):
    cells = x.shape[3]
    x = x.reshape(2, NV, NV, cells // (8 * LANES), 8, LANES).transpose(1, 2, 3, 4, 0, 5)
    return x.reshape(NV, NV, cells // (8 * LANES), 16, LANES)


def shards(adjoint, jacobian, source_term, face_area, face_band, partition_row):
    cells, faces = adjoint.shape[2], face_area.shape[0]
    groups = cells // (4 * LANES)
    assert groups == GROUPS
    f32, bf16, i32 = jnp.float32, jnp.bfloat16, jnp.int32
    dma = pltpu.SemaphoreType.DMA
    state = pltpu.VMEM((NV, groups, 8, LANES), f32)
    box = pltpu.VMEM((16, LANES), f32)
    boxes = pltpu.VMEM((OWNERS, 16, LANES), f32)
    updated = pl.pallas_call(
        kernel,
        out_shape=pltpu.VMEM((NV, groups, 8, LANES), f32),
        in_specs=[pl.BlockSpec(memory_space=pl.ANY)] * 5 + [pl.BlockSpec(memory_space=pltpu.SMEM)],
        out_specs=pl.BlockSpec(memory_space=pltpu.VMEM),
        scratch_shapes=[
            state,
            pltpu.VMEM((NV, NV, groups // 2, 16, LANES), bf16),
            state,
            state,
            pltpu.VMEM((2 * PARTS, NV, PART, 8, LANES), f32),
            pltpu.VMEM((PARTS, NV, PART, 8, LANES), f32),
            pltpu.VMEM((NV, RAW, 8, LANES), f32),
            pltpu.VMEM((NV, RAW, 8, LANES), f32),
            pltpu.VMEM((faces // LANES, LANES), f32),
            pltpu.VMEM((faces // LANES, LANES), i32),
            pltpu.VMEM((faces, BANDS), bf16),
            pltpu.VMEM((faces // (4 * LANES), 8, LANES), i32),
            pltpu.VMEM((24, faces), f32),
            boxes,
            boxes,
            box,
            box,
            box,
            pltpu.VMEM((OWNERS // 2, 16, LANES), f32),
            pltpu.VMEM((NV * (3 * GROUPS + RAW), 8, LANES), f32),
            pltpu.SemaphoreType.REGULAR,
            dma((6,)),
            dma,
            dma((3,)),
            dma,
            dma((2,)),
            dma,
            dma,
            dma,
            dma,
        ],
        compiler_params=pltpu.CompilerParams(
            collective_id=0, has_side_effects=True, vmem_limit_bytes=40 << 20
        ),
    )(
        hbm(fold(adjoint)),
        hbm(fold_jacobian(jacobian)),
        hbm(fold(source_term)),
        hbm(face_area.reshape(faces // LANES, LANES)),
        hbm(face_band.reshape(faces // LANES, LANES)),
        partition_row,
    )
    return unfold(updated)


def solution(mesh):
    placed = (
        P("inst", None, "rows"),
        P("inst", None, None, "rows"),
        P("inst", None, "rows"),
        P("rows"),
        P("rows"),
        P("rows"),
    )
    return jax.shard_map(
        shards, mesh=mesh, in_specs=placed, out_specs=P("inst", None, "rows"), check_vma=False
    )
```
